1024 devices in a mesh: dp: 4 (over z_lo, core), expert: 64 (over y, x), tensor: 4 (over z_hi).
Axes of the slice: x: 8, y: 8, z: 8 (z_hi: 4, z_lo: 2; z = z_hi * 2 + z_lo), core: 2. Of those that a mesh axis runs over, the one named last changes fastest.
Arguments:
- attn_out: bfloat16 [2048, 16384], P(('dp', 'expert'), 'tensor'), parts along dimension 0, may hold values from -6 to 6
- w_proj: bfloat16 [16384, 7168], P('tensor', 'expert'), may hold values from -0.046875 to 0.046875
- w_in: bfloat16 [64, 7168, 2, 512], P('expert', 'tensor'), may hold values from -0.0625 to 0.0625
- w_out: bfloat16 [64, 512, 7168], P('expert', None, 'tensor'), may hold values from -0.125 to 0.125
- expert_ids: int32 [2048, 8], P(('dp', 'expert')), parts along dimension 0, may hold values from 0 to 255, as said below
- slots: int32 [2048, 8], P(('dp', 'expert')), parts along dimension 0, may hold values from -1 to 1, as said below
- gates: float32 [2048, 8], P(('dp', 'expert')), parts along dimension 0, may hold values from 0.2 to 1
Outputs:
- projected: bfloat16 [2048, 7168], P(('dp', 'expert'), 'tensor'), parts along dimension 0
- moe_out: bfloat16 [2048, 7168], P(('dp', 'expert'), 'tensor'), parts along dimension 0
The draws below stay inside these ranges and needn't reach their ends.
There are 4 independent parts, one for each index of `dp`. The reference program is written for one: setup_inputs(seed, part) draws one part's arguments, and reference() takes and returns one part's arrays. A program takes and returns all parts, laid end to end along the dimension named above; an argument that names none is the same for every part. Nothing has to cross between parts.
Inputs may be any that keep to these rules, and one draw needn't show every extreme that they name: `expert_ids`: each row names 8 different experts. Within each aligned block of 8 rows, the picks of one expert that are not dropped hold the slots 0, 1, ... in order of the rows, and a pick is dropped only when 2 earlier picks of its block already name the same expert. In every block some expert of the wave fills all 2 slots.
All inputs are finite; a program needn't handle non-finite values.
Results may differ from the reference program's by a relative error of at most 0.012.
Values may be sent and summed in bfloat16 or wider, within the bound.
No kernel may reach another device: no remote copies, remote signals or barrier semaphores. Data moves between devices by JAX's collectives and lax.ppermute only.
A program may use at most 32 MiB of HBM per device.

```python
import jax
import jax.numpy as jnp
from jax import lax

D = 7168
HEADS = 128
HEAD_DIM = 128
HID = 2048
EXPERTS = 256
TOPK = 8
HSPLIT = 4
CAP = 2
TOK_DEV = 8
HS = 512
TOKENS = 512
FLIGHT = 16
SLICES = 64


def routing_table(key):
    key_noise, key_lift, key_hot = jax.random.split(key, 3)
    experts_range = jnp.arange(EXPERTS, dtype=jnp.int32)
    noise = jax.random.randint(key_noise, (TOKENS, EXPERTS), 0, 2 ** 20, dtype=jnp.int32)
    lift = jax.random.randint(key_lift, (EXPERTS,), 0, 2 ** 19, dtype=jnp.int32)
    lift = jnp.where(experts_range < FLIGHT, lift, 0)
    hottest = jax.random.randint(key_hot, (), 0, FLIGHT, dtype=jnp.int32)
    lift = lift + jnp.where(experts_range == hottest, 2 ** 21, 0)
    score = (noise + lift) * EXPERTS + experts_range
    _, picked = lax.top_k(score, TOPK)
    picked = picked.astype(jnp.int32)
    onehot = jnp.sum((picked[:, :, None] == experts_range).astype(jnp.int32), axis=1)
    blocked = onehot.reshape(TOKENS // TOK_DEV, TOK_DEV, EXPERTS)
    prior = (jnp.cumsum(blocked, axis=1) - blocked).reshape(TOKENS, EXPERTS)
    ranked = jnp.take_along_axis(prior, picked, axis=1)
    slot_vals = jnp.where(ranked < CAP, ranked, -1).astype(jnp.int32)
    return (picked, slot_vals)


def draw_expert_ids(key, part):
    return routing_table(key)[0]


def draw_slots(key, part):
    return routing_table(key)[1]


def shard_levels(stream_key, shape, cuts, smallest, largest):
    loudness = 1.0
    for axis_at, blocks in cuts:
        heights = jax.random.uniform(jax.random.fold_in(jax.random.fold_in(stream_key, 6), axis_at), (blocks,), jnp.float32, smallest / len(cuts), largest / len(cuts))
        loudness = loudness * jnp.repeat(jnp.exp(heights), shape[axis_at] // blocks).reshape((-1,) + (1,) * (len(shape) - 1 - axis_at))
    return loudness


def scatter_about(stream_key, shape, deviation, limit, shards=(), held_as=jnp.bfloat16):
    drawn = deviation * jax.random.normal(stream_key, shape, jnp.float32)
    if shards:
        drawn = drawn * shard_levels(stream_key, shape, shards, -0.22, 0.18)
    return jnp.clip(drawn, -limit, limit).astype(held_as)


def setup_inputs(seed: int = 0, part: int = 0) -> dict:
    key_of = jax.random.split(jax.random.key(seed), 8)
    own_keys = jax.random.split(jax.random.fold_in(key_of[7], part), 8)
    attn_out = scatter_about(own_keys[0], (TOKENS, HEADS * HEAD_DIM), 1.0, 6.0, ((0, 64), (1, 4)))
    w_proj = scatter_about(key_of[1], (HEADS * HEAD_DIM, D), (HEADS * HEAD_DIM) ** -0.5, 0.046875, ((0, 4), (1, 64)))
    w_in = scatter_about(key_of[2], (SLICES, D, 2, HS), D ** -0.5, 0.0625, ((0, 64), (1, 4)))
    w_out = scatter_about(key_of[3], (SLICES, HS, D), HID ** -0.5, 0.125, ((0, 64), (2, 4)))
    expert_ids = draw_expert_ids(jax.random.fold_in(jax.random.fold_in(key_of[7], part), 71), part)
    slots = draw_slots(jax.random.fold_in(jax.random.fold_in(key_of[7], part), 71), part)
    gates = jnp.clip(0.2 + 0.8 * jax.random.uniform(own_keys[6], (TOKENS, TOPK), jnp.float32) ** shard_levels(own_keys[6], (TOKENS, TOPK), ((0, 64),), -0.2, 0.2), 0.2, 1.0)
    return {"attn_out": attn_out, "w_proj": w_proj, "w_in": w_in, "w_out": w_out, "expert_ids": expert_ids, "slots": slots, "gates": gates}


def reference(attn_out, w_proj, w_in, w_out, expert_ids, slots, gates):
    projected = jnp.dot(attn_out, w_proj, preferred_element_type=jnp.float32).astype(jnp.bfloat16)
    blocks = TOKENS // TOK_DEV
    blocked = projected.reshape(blocks, TOK_DEV, D).astype(jnp.float32)
    ids_blocked = expert_ids.reshape(blocks, TOK_DEV, TOPK)
    slots_blocked = slots.reshape(blocks, TOK_DEV, TOPK)
    gates_blocked = gates.reshape(blocks, TOK_DEV, TOPK)
    slot_range = jnp.arange(CAP, dtype=jnp.int32)
    weights_in = w_in.reshape(FLIGHT, HSPLIT, D, 2, HS)
    weights_out = w_out.reshape(FLIGHT, HID, D)

    def add_expert(total, expert):
        matched = (ids_blocked == expert)[..., None] & (slots_blocked[..., None] == slot_range)
        dispatch_w = jnp.sum(matched.astype(jnp.float32), axis=2)
        combine_w = jnp.sum(jnp.where(matched, gates_blocked[..., None], jnp.float32(0.0)), axis=2)
        routed = jnp.einsum("btc,btd->bcd", dispatch_w, blocked, precision=lax.Precision.HIGHEST)
        routed = routed.astype(jnp.bfloat16).reshape(blocks * CAP, D)
        chosen = lax.dynamic_index_in_dim(weights_in, expert, 0, keepdims=False)
        gate_w = jnp.transpose(chosen[:, :, 0, :], (1, 0, 2)).reshape(D, HID)
        up_w = jnp.transpose(chosen[:, :, 1, :], (1, 0, 2)).reshape(D, HID)
        gate_val = jnp.dot(routed, gate_w, preferred_element_type=jnp.float32)
        up_val = jnp.dot(routed, up_w, preferred_element_type=jnp.float32)
        hidden = (jax.nn.silu(gate_val) * up_val).astype(jnp.bfloat16)
        down_w = lax.dynamic_index_in_dim(weights_out, expert, 0, keepdims=False)
        expert_out = jnp.dot(hidden, down_w, preferred_element_type=jnp.float32).reshape(blocks, CAP, D)
        added = jnp.einsum("btc,bcd->btd", combine_w, expert_out, precision=lax.Precision.HIGHEST)
        return total + added, None

    start = jnp.zeros((blocks, TOK_DEV, D), jnp.float32)
    total, _ = lax.scan(add_expert, start, jnp.arange(FLIGHT, dtype=jnp.int32))
    return projected, total.reshape(TOKENS, D).astype(jnp.bfloat16)
```

```python
import jax
import jax.numpy as jnp
from jax import lax
from jax.sharding import Mesh, PartitionSpec as P

HSPLIT = 4
CAP = 2
EXPERT = ("yh", "yl", "xh", "xl")
TURNED = ("tensor", "yl", "xh", "xl")
BF16 = jnp.bfloat16
F32 = jnp.float32


def project(attn_out, w_proj):
    rows, depth = attn_out.shape
    cols = w_proj.shape[1]
    part = depth // 4
    me = lax.axis_index(("yl", "xl"))
    w_cols = w_proj.T
    blocks = []
    for d in range(4):
        piece = lax.dynamic_slice(w_cols, (0, (me ^ d) * part), (cols, part))
        if d:
            piece = lax.ppermute(piece, ("yl", "xl"), [(i, i ^ d) for i in range(4)])
        blocks.append(piece)
    sent = attn_out.reshape(rows, 2, 2, part).transpose(1, 2, 0, 3)
    sent = jnp.broadcast_to(sent[None, :, None, :], (4, 2, 4, 2, rows, part))
    tokens = lax.all_to_all(
        sent.reshape(64, rows, part), EXPERT, split_axis=0, concat_axis=0, tiled=True
    ).reshape(64 * rows, part)
    wide = jnp.zeros((4, cols, part), BF16)
    for d in range(4):
        wide = lax.dynamic_update_slice(wide, blocks[d][None], (me ^ d, 0, 0))
    partial = lax.dot_general(
        tokens, wide.reshape(4 * cols, part), (((1,), (1,)), ((), ())), preferred_element_type=F32
    ).astype(BF16)
    got = lax.all_to_all(
        partial.reshape(64, rows, 4 * cols), TURNED, split_axis=0, concat_axis=0, tiled=True
    )
    got = got.reshape(4, 2, 4, 2, rows, 4 * cols).astype(F32)
    total = jnp.sum(got, axis=(0, 1, 3)).astype(BF16)
    total = total.reshape(4, rows, 2, 2, cols).transpose(1, 2, 0, 3, 4).reshape(rows, 16 * cols)
    return lax.ppermute(
        total, ("yh", "tensor"), [(a * 4 + b, b * 4 + a) for a in range(4) for b in range(4)]
    )


def per_device(attn_out, w_proj, w_in, w_out, expert_ids, slots, gates):
    groups = lax.axis_size(EXPERT)
    flight = groups // HSPLIT
    width_block = w_in.shape[1]
    slice_units = w_in.shape[3]
    wave_pos = jnp.arange(flight * CAP, dtype=jnp.int32)
    matches = (expert_ids[:, :, None] == wave_pos // CAP) & (slots[:, :, None] == wave_pos % CAP)
    dispatch_w = jnp.sum(matches.astype(F32), axis=1).astype(BF16)
    combine_w = jnp.sum(jnp.where(matches, gates[:, :, None], F32(0.0)), axis=1)
    projected = project(attn_out, w_proj)
    routed = jnp.einsum("tw,td->wd", dispatch_w, projected, preferred_element_type=F32)
    routed = routed.astype(BF16).reshape(flight, 1, CAP, width_block)
    outgoing = jnp.broadcast_to(routed, (flight, HSPLIT, CAP, width_block)).reshape(
        groups, CAP, width_block
    )
    gate_up_w = w_in.reshape(width_block, 2 * slice_units)
    down_w = w_out.reshape(slice_units, width_block)
    received = lax.all_to_all(outgoing, EXPERT, split_axis=0, concat_axis=0, tiled=True)
    flat_rows = received.reshape(groups * CAP, width_block)
    gate_up = jnp.dot(flat_rows, gate_up_w, preferred_element_type=F32).astype(BF16)
    quarter = groups * CAP // 4
    gate_up = lax.all_to_all(
        gate_up.reshape(4, quarter, 2 * slice_units), "tensor", split_axis=0, concat_axis=0, tiled=True
    )
    gate_up = jnp.sum(gate_up.astype(F32), axis=0)
    hidden = (jax.nn.silu(gate_up[:, :slice_units]) * gate_up[:, slice_units:]).astype(BF16)
    hidden = lax.all_to_all(
        jnp.broadcast_to(hidden[None], (4, quarter, slice_units)),
        "tensor",
        split_axis=0,
        concat_axis=0,
        tiled=True,
    ).reshape(groups * CAP, slice_units)
    result = jnp.dot(hidden, down_w, preferred_element_type=F32)
    returned = lax.all_to_all(
        result.reshape(groups, CAP, width_block).astype(BF16),
        EXPERT,
        split_axis=0,
        concat_axis=0,
        tiled=True,
    ).astype(F32)
    expert_sum = jnp.sum(returned.reshape(flight, HSPLIT, CAP, width_block), axis=1)
    expert_sum = expert_sum.reshape(flight * CAP, width_block)
    moe_out = jnp.dot(
        combine_w, expert_sum, precision=lax.Precision.HIGHEST, preferred_element_type=F32
    )
    return (projected, moe_out.astype(BF16))


def solution(mesh):
    split = Mesh(
        mesh.devices.reshape(4, 4, 2, 4, 2, 4), ("dp", "yh", "yl", "xh", "xl", "tensor")
    )
    rows = ("dp",) + EXPERT
    placed = (
        P(rows, "tensor"),
        P("tensor", EXPERT),
        P(EXPERT, "tensor", None, None),
        P(EXPERT, None, "tensor"),
        P(rows, None),
        P(rows, None),
        P(rows, None),
    )
    return jax.shard_map(
        per_device,
        mesh=split,
        in_specs=placed,
        out_specs=(P(rows, "tensor"), P(rows, "tensor")),
        check_vma=False,
    )
```

```python
import jax
import jax.numpy as jnp
from jax import lax
from jax.experimental import pallas as pl
from jax.experimental.pallas import tpu as pltpu
from jax.sharding import Mesh, PartitionSpec as P

HSPLIT = 4
CAP = 2
EXPERT = ("yh", "yl", "xh", "xl")
TURNED = ("tensor", "yl", "xh", "xl")
BF16 = jnp.bfloat16
F32 = jnp.float32


def pack_kernel(where, attn_ref, w_ref, sent_ref, *refs):
    pieces, own_ref, (staged, sems) = refs[:3], refs[3], refs[4:]
    part = attn_ref.shape[1] // 4
    half = part // 2
    me, core = where[0], where[1]
    copies = []
    for d in range(1, 4):
        start = pl.multiple_of((me ^ d) * part + core * half, half)
        copies.append(
            pltpu.make_async_copy(w_ref.at[:, pl.ds(start, half)], pieces[d - 1], sems.at[d - 1])
        )
        copies[-1].start()
    start = pl.multiple_of(me * part, part)
    copies.append(pltpu.make_async_copy(w_ref.at[:, pl.ds(start, part)], own_ref, sems.at[7]))
    copies[-1].start()
    for yl in range(2):
        for x in range(8):
            m = yl * 2 + x % 2
            staged[yl * 8 + x] = attn_ref[:, m * part : (m + 1) * part]
    for yh in range(4):
        copies.append(
            pltpu.make_async_copy(staged, sent_ref.at[pl.ds(yh * 16, 16)], sems.at[3 + yh])
        )
        copies[-1].start()
    for copy in copies:
        copy.wait()


def pack(where, attn_out, w_cols):
    rows, depth = attn_out.shape
    cols, part = w_cols.shape[0], depth // 4
    return pl.pallas_call(
        pack_kernel,
        out_shape=[jax.ShapeDtypeStruct((64, rows, part), BF16)]
        + [jax.ShapeDtypeStruct((cols, part // 2), BF16)] * 3
        + [jax.ShapeDtypeStruct((cols, part), BF16)],
        in_specs=[
            pl.BlockSpec(memory_space=pltpu.SMEM),
            pl.BlockSpec(memory_space=pltpu.VMEM),
            pl.BlockSpec(memory_space=pl.ANY),
        ],
        out_specs=[pl.BlockSpec(memory_space=pl.ANY)] * 5,
        scratch_shapes=[pltpu.VMEM((16, rows, part), BF16), pltpu.SemaphoreType.DMA((8,))],
        compiler_params=pltpu.CompilerParams(vmem_limit_bytes=58 << 20),
        name="pack",
    )(where, attn_out, w_cols)


def partial_kernel(where, tokens, own, *refs):
    mine, other, (out_ref, wide, sems) = refs[:3], refs[3:6], refs[6:]
    cols, half = mine[0].shape
    me, core = where[0], where[1]
    copies = []

    def bring(src, d, lane, width):
        row = pl.multiple_of((me ^ d) * cols, 16)
        copies.append(
            pltpu.make_async_copy(
                src, wide.at[pl.ds(row, cols), pl.ds(lane, width)], sems.at[len(copies)]
            )
        )
        copies[-1].start()

    bring(own, 0, 0, 2 * half)
    for d in range(1, 4):
        bring(mine[d - 1], d, pl.multiple_of(core * half, half), half)
        bring(other[d - 1], d, pl.multiple_of((1 - core) * half, half), half)
    for copy in copies:
        copy.wait()
    step = 128
    for i in range(tokens.shape[0] // step):
        at = pl.ds(i * step, step)
        out_ref[at, :] = lax.dot_general(
            tokens[at, :], wide[...], (((1,), (1,)), ((), ())), preferred_element_type=F32
        ).astype(BF16)


def partial_sums(where, tokens, own, mine, other):
    cols = own.shape[0]
    return pl.pallas_call(
        partial_kernel,
        out_shape=jax.ShapeDtypeStruct((tokens.shape[0], 4 * cols), BF16),
        in_specs=[
            pl.BlockSpec(memory_space=pltpu.SMEM),
            pl.BlockSpec(memory_space=pltpu.VMEM),
            pl.BlockSpec(memory_space=pl.ANY),
        ]
        + [pl.BlockSpec(memory_space=pl.ANY)] * 6,
        out_specs=pl.BlockSpec(memory_space=pltpu.VMEM),
        scratch_shapes=[
            pltpu.VMEM((4 * cols, tokens.shape[1]), BF16),
            pltpu.SemaphoreType.DMA((7,)),
        ],
        compiler_params=pltpu.CompilerParams(vmem_limit_bytes=8 << 20),
        name="partial_sums",
    )(where, tokens, own, *mine, *other)


def project(attn_out, w_proj):
    rows = attn_out.shape[0]
    cols = w_proj.shape[1]
    w_cols = w_proj.T
    where = jnp.stack([lax.axis_index(("yl", "xl")), lax.axis_index("core")]).astype(jnp.int32)
    sent, *pieces, own = pack(where, attn_out, w_cols)
    tokens = lax.all_to_all(sent, EXPERT, split_axis=0, concat_axis=0, tiled=True)
    mine = [
        lax.ppermute(pieces[d - 1], ("yl", "xl"), [(i, i ^ d) for i in range(4)])
        for d in range(1, 4)
    ]
    other = [lax.ppermute(piece, "core", [(0, 1), (1, 0)]) for piece in mine]
    partial = partial_sums(where, tokens.reshape(64 * rows, -1), own, mine, other)
    got = lax.all_to_all(
        partial.reshape(64, rows, 4 * cols), TURNED, split_axis=0, concat_axis=0, tiled=True
    )
    got = got.reshape(4, 2, 4, 2, rows, 4 * cols).astype(F32)
    total = jnp.sum(got, axis=(0, 1, 3)).astype(BF16)
    total = total.reshape(4, rows, 2, 2, cols).transpose(1, 2, 0, 3, 4).reshape(rows, 16 * cols)
    return lax.ppermute(
        total, ("yh", "tensor"), [(a * 4 + b, b * 4 + a) for a in range(4) for b in range(4)]
    )


def per_device(attn_out, w_proj, w_in, w_out, expert_ids, slots, gates):
    groups = lax.axis_size(EXPERT)
    width_block = w_in.shape[1]
    slice_units = w_in.shape[3]
    row = jnp.arange(groups * CAP, dtype=jnp.int32)
    matches = (expert_ids[:, :, None] == row // (HSPLIT * CAP)) & (slots[:, :, None] == row % CAP)
    dispatch_w = jnp.sum(matches.astype(F32), axis=1).astype(BF16)
    combine_w = jnp.sum(jnp.where(matches, gates[:, :, None], F32(0.0)), axis=1)
    combine_hi = lax.reduce_precision(combine_w, 8, 7)
    combine_w = jnp.concatenate([combine_hi, combine_w - combine_hi], axis=0).astype(BF16)
    projected = project(attn_out, w_proj)
    outgoing = jnp.einsum(
        "tgc,td->gcd",
        dispatch_w.reshape(-1, groups, CAP),
        projected,
        preferred_element_type=F32,
    ).astype(BF16)
    gate_up_w = w_in.reshape(width_block, 2 * slice_units)
    down_w = w_out.reshape(slice_units, width_block)
    received = lax.all_to_all(outgoing, EXPERT, split_axis=0, concat_axis=0, tiled=True)
    flat_rows = received.reshape(groups * CAP, width_block)
    gate_up = jnp.dot(flat_rows, gate_up_w, preferred_element_type=F32).astype(BF16)
    quarter = groups * CAP // 4
    gate_up = lax.all_to_all(
        gate_up.reshape(4, quarter, 2 * slice_units), "tensor", split_axis=0, concat_axis=0, tiled=True
    )
    gate_up = jnp.sum(gate_up.astype(F32), axis=0)
    hidden = (jax.nn.silu(gate_up[:, :slice_units]) * gate_up[:, slice_units:]).astype(BF16)
    hidden = lax.all_to_all(
        jnp.broadcast_to(hidden[None], (4, quarter, slice_units)),
        "tensor",
        split_axis=0,
        concat_axis=0,
        tiled=True,
    ).reshape(groups * CAP, slice_units)
    result = jnp.dot(hidden, down_w, preferred_element_type=F32)
    returned = lax.all_to_all(
        result.reshape(groups, CAP, width_block).astype(BF16),
        EXPERT,
        split_axis=0,
        concat_axis=0,
        tiled=True,
    ).reshape(groups * CAP, width_block)
    moe_out = jnp.dot(combine_w, returned, preferred_element_type=F32)
    moe_out = jnp.sum(moe_out.reshape(2, -1, width_block), axis=0)
    return (projected, moe_out.astype(BF16))


def solution(mesh):
    split = Mesh(
        mesh.devices.reshape(2, 2, 4, 2, 4, 2, 4),
        ("plane", "core", "yh", "yl", "xh", "xl", "tensor"),
    )
    rows = ("plane", "core") + EXPERT
    placed = (
        P(rows, "tensor"),
        P("tensor", EXPERT),
        P(EXPERT, "tensor", None, None),
        P(EXPERT, None, "tensor"),
        P(rows, None),
        P(rows, None),
        P(rows, None),
    )
    return jax.shard_map(
        per_device,
        mesh=split,
        in_specs=placed,
        out_specs=(P(rows, "tensor"), P(rows, "tensor")),
        check_vma=False,
    )
```

```python
import jax
import jax.numpy as jnp
from jax import lax
from jax.experimental import pallas as pl
from jax.experimental.pallas import tpu as pltpu
from jax.sharding import Mesh, PartitionSpec as P

HSPLIT = 4
CAP = 2
EXPERT = ("yh", "yl", "xh", "xl")
TURNED = ("tensor", "yl", "xh", "xl")
BF16 = jnp.bfloat16
F32 = jnp.float32


def pack_kernel(attn_ref, w_ref, sent_ref, pieces_ref, staged, sems):
    part = attn_ref.shape[1] // 4
    for m in range(4):
        block = attn_ref[:, m * part : (m + 1) * part]
        for x in range(4):
            staged[(m // 2) * 8 + x * 2 + m % 2] = block
    copies = [
        pltpu.make_async_copy(staged, sent_ref.at[pl.ds(yh * 16, 16)], sems.at[yh])
        for yh in range(4)
    ]
    for copy in copies:
        copy.start()
    for m in range(4):
        pieces_ref[m] = w_ref[:, m * part : (m + 1) * part]
    for copy in copies:
        copy.wait()


def pack(attn_out, w_cols):
    rows, depth = attn_out.shape
    cols, part = w_cols.shape[0], depth // 4
    vmem = pl.BlockSpec(memory_space=pltpu.VMEM)
    return pl.pallas_call(
        pack_kernel,
        out_shape=[
            jax.ShapeDtypeStruct((64, rows, part), BF16),
            jax.ShapeDtypeStruct((4, cols, part), BF16),
        ],
        in_specs=[vmem, vmem],
        out_specs=[pl.BlockSpec(memory_space=pl.ANY), vmem],
        scratch_shapes=[pltpu.VMEM((16, rows, part), BF16), pltpu.SemaphoreType.DMA((4,))],
        compiler_params=pltpu.CompilerParams(vmem_limit_bytes=16 << 20),
        name="pack",
    )(attn_out, w_cols)


def partial_kernel(tokens, wide, out_ref):
    out_ref[...] = lax.dot_general(
        tokens[...], wide[...], (((1,), (1,)), ((), ())), preferred_element_type=F32
    ).astype(BF16)


def partial_sums(tokens, wide):
    vmem = pl.BlockSpec(memory_space=pltpu.VMEM)
    return pl.pallas_call(
        partial_kernel,
        out_shape=jax.ShapeDtypeStruct((tokens.shape[0], wide.shape[0]), BF16),
        in_specs=[vmem, vmem],
        out_specs=vmem,
        compiler_params=pltpu.CompilerParams(vmem_limit_bytes=16 << 20),
        name="partial_sums",
    )(tokens, wide)


def project(attn_out, w_proj, gate_up_w):
    rows, cols = attn_out.shape[0], w_proj.shape[1]
    sent, pieces = pack(attn_out, w_proj.T)
    wide = lax.all_to_all(pieces, ("yl", "xl"), split_axis=0, concat_axis=0, tiled=True)
    sent, wide = lax.optimization_barrier((sent, wide))
    tokens = lax.all_to_all(sent, EXPERT, split_axis=0, concat_axis=0, tiled=True)
    tokens, gate_up_w = lax.optimization_barrier((tokens, gate_up_w))
    partial = partial_sums(tokens.reshape(64 * rows, -1), wide.reshape(4 * cols, -1))
    got = lax.all_to_all(
        partial.reshape(64, rows, 4 * cols), TURNED, split_axis=0, concat_axis=0, tiled=True
    )
    got = got.reshape(4, 2, 4, 2, rows, 4 * cols).astype(F32)
    total = jnp.sum(got, axis=(0, 1, 3)).astype(BF16)
    total = total.reshape(4, rows, 2, 2, cols).transpose(1, 2, 0, 3, 4).reshape(rows, 16 * cols)
    turned = lax.ppermute(
        total, ("yh", "tensor"), [(a * 4 + b, b * 4 + a) for a in range(4) for b in range(4)]
    )
    return turned, gate_up_w


def per_device(attn_out, w_proj, w_in, w_out, expert_ids, slots, gates):
    groups = lax.axis_size(EXPERT)
    width_block = w_in.shape[1]
    slice_units = w_in.shape[3]
    row = jnp.arange(groups * CAP, dtype=jnp.int32)
    matches = (expert_ids[:, :, None] == row // (HSPLIT * CAP)) & (slots[:, :, None] == row % CAP)
    dispatch_w = jnp.sum(matches.astype(F32), axis=1).astype(BF16)
    combine_w = jnp.sum(jnp.where(matches, gates[:, :, None], F32(0.0)), axis=1)
    projected, gate_up_w = project(attn_out, w_proj, w_in.reshape(width_block, 2 * slice_units))
    outgoing = jnp.einsum(
        "tgc,td->gcd",
        dispatch_w.reshape(-1, groups, CAP),
        projected,
        preferred_element_type=F32,
    ).astype(BF16)
    down_w = w_out.reshape(slice_units, width_block)
    received = lax.all_to_all(outgoing, EXPERT, split_axis=0, concat_axis=0, tiled=True)
    flat_rows = received.reshape(groups * CAP, width_block)
    gate_up = jnp.dot(flat_rows, gate_up_w, preferred_element_type=F32).astype(BF16)
    quarter = groups * CAP // 4
    gate_up = lax.all_to_all(
        gate_up.reshape(4, quarter, 2 * slice_units), "tensor", split_axis=0, concat_axis=0, tiled=True
    )
    gate_up = jnp.sum(gate_up.astype(F32), axis=0)
    hidden = (jax.nn.silu(gate_up[:, :slice_units]) * gate_up[:, slice_units:]).astype(BF16)
    hidden = lax.all_to_all(
        jnp.broadcast_to(hidden[None], (4, quarter, slice_units)),
        "tensor",
        split_axis=0,
        concat_axis=0,
        tiled=True,
    ).reshape(groups * CAP, slice_units)
    result = jnp.dot(hidden, down_w, preferred_element_type=F32)
    returned = lax.all_to_all(
        result.reshape(groups, CAP, width_block).astype(BF16),
        EXPERT,
        split_axis=0,
        concat_axis=0,
        tiled=True,
    ).reshape(groups * CAP, width_block)
    moe_out = jnp.dot(
        combine_w, returned.astype(F32), precision=lax.Precision.HIGHEST, preferred_element_type=F32
    )
    return (projected, moe_out.astype(BF16))


def solution(mesh):
    split = Mesh(
        mesh.devices.reshape(2, 2, 4, 2, 4, 2, 4),
        ("plane", "core", "yh", "yl", "xh", "xl", "tensor"),
    )
    rows = ("plane", "core") + EXPERT
    placed = (
        P(rows, "tensor"),
        P("tensor", EXPERT),
        P(EXPERT, "tensor", None, None),
        P(EXPERT, None, "tensor"),
        P(rows, None),
        P(rows, None),
        P(rows, None),
    )
    return jax.shard_map(
        per_device,
        mesh=split,
        in_specs=placed,
        out_specs=(P(rows, "tensor"), P(rows, "tensor")),
        check_vma=False,
    )
```

```python
import jax
import jax.numpy as jnp
from jax import lax
from jax.experimental import pallas as pl
from jax.experimental.pallas import tpu as pltpu
from jax.sharding import Mesh, PartitionSpec as P

HSPLIT = 4
CAP = 2
EXPERT = ("yh", "yl", "xh", "xl")
TURNED = ("tensor", "yl", "xh", "xl")
BF16 = jnp.bfloat16
F32 = jnp.float32


VMEM = pl.BlockSpec(memory_space=pltpu.VMEM)
SMEM = pl.BlockSpec(memory_space=pltpu.SMEM)
ANY = pl.BlockSpec(memory_space=pl.ANY)


def address_kernel(attn_ref, sent_ref, staged, in_sems, out_sems):
    part = attn_ref.shape[1] // 4
    copies = []
    for m in range(4):
        for x in range(4):
            at = (m // 2) * 8 + x * 2 + m % 2
            copies.append(
                pltpu.make_async_copy(
                    attn_ref.at[:, pl.ds(m * part, part)], staged.at[at], in_sems.at[at]
                )
            )
    for copy in copies:
        copy.start()
    for copy in copies:
        copy.wait()
    copies = [
        pltpu.make_async_copy(staged, sent_ref.at[pl.ds(yh * 16, 16)], out_sems.at[yh])
        for yh in range(4)
    ]
    for copy in copies:
        copy.start()
    for copy in copies:
        copy.wait()


def address(attn_out):
    rows, part = attn_out.shape[0], attn_out.shape[1] // 4
    return pl.pallas_call(
        address_kernel,
        out_shape=jax.ShapeDtypeStruct((64, rows, part), BF16),
        in_specs=[ANY],
        out_specs=ANY,
        scratch_shapes=[
            pltpu.VMEM((16, rows, part), BF16),
            pltpu.SemaphoreType.DMA((16,)),
            pltpu.SemaphoreType.DMA((4,)),
        ],
        compiler_params=pltpu.CompilerParams(vmem_limit_bytes=58 << 20),
        name="address",
    )(attn_out)


def cut_kernel(me, w_ref, *pieces):
    part = pieces[0].shape[1]
    for d in range(4):
        start = pl.multiple_of((me[0] ^ d) * part, part)
        pieces[d][...] = w_ref[:, pl.ds(start, part)]


def cut(me, w_cols):
    cols, part = w_cols.shape[0], w_cols.shape[1] // 4
    return pl.pallas_call(
        cut_kernel,
        out_shape=[jax.ShapeDtypeStruct((cols, part), BF16)] * 4,
        in_specs=[SMEM, VMEM],
        out_specs=[VMEM] * 4,
        compiler_params=pltpu.CompilerParams(vmem_limit_bytes=8 << 20),
        name="cut",
    )(me, w_cols)


def partial_kernel(me, tokens, *refs):
    blocks, (out_ref, wide) = refs[:4], refs[4:]
    cols = blocks[0].shape[0]
    for d in range(4):
        wide[pl.ds(pl.multiple_of((me[0] ^ d) * cols, 16), cols), :] = blocks[d][...]
    out_ref[...] = lax.dot_general(
        tokens[...], wide[...], (((1,), (1,)), ((), ())), preferred_element_type=F32
    ).astype(BF16)


def partial_sums(me, tokens, blocks):
    cols, part = blocks[0].shape
    return pl.pallas_call(
        partial_kernel,
        out_shape=jax.ShapeDtypeStruct((tokens.shape[0], 4 * cols), BF16),
        in_specs=[SMEM] + [VMEM] * 5,
        out_specs=VMEM,
        scratch_shapes=[pltpu.VMEM((4 * cols, part), BF16)],
        compiler_params=pltpu.CompilerParams(vmem_limit_bytes=16 << 20),
        name="partial_sums",
    )(me, tokens, *blocks)


def project(attn_out, w_proj, gate_up_w):
    rows, cols = attn_out.shape[0], w_proj.shape[1]
    me = lax.axis_index(("yl", "xl")).reshape(1).astype(jnp.int32)
    tokens = lax.all_to_all(address(attn_out), EXPERT, split_axis=0, concat_axis=0, tiled=True)
    blocks = list(cut(me, w_proj.T))
    for d in range(1, 4):
        blocks[d] = lax.ppermute(blocks[d], ("yl", "xl"), [(i, i ^ d) for i in range(4)])
    tokens, gate_up_w = lax.optimization_barrier((tokens, gate_up_w))
    partial = partial_sums(me, tokens.reshape(64 * rows, -1), blocks)
    got = lax.all_to_all(
        partial.reshape(64, rows, 4 * cols), TURNED, split_axis=0, concat_axis=0, tiled=True
    )
    got = got.reshape(4, 2, 4, 2, rows, 4 * cols).astype(F32)
    total = jnp.sum(got, axis=(0, 1, 3)).astype(BF16)
    total = total.reshape(4, rows, 2, 2, cols).transpose(1, 2, 0, 3, 4).reshape(rows, 16 * cols)
    turned = lax.ppermute(
        total, ("yh", "tensor"), [(a * 4 + b, b * 4 + a) for a in range(4) for b in range(4)]
    )
    return turned, gate_up_w


def per_device(attn_out, w_proj, w_in, w_out, expert_ids, slots, gates):
    groups = lax.axis_size(EXPERT)
    width_block = w_in.shape[1]
    slice_units = w_in.shape[3]
    row = jnp.arange(groups * CAP, dtype=jnp.int32)
    matches = (expert_ids[:, :, None] == row // (HSPLIT * CAP)) & (slots[:, :, None] == row % CAP)
    dispatch_w = jnp.sum(matches.astype(F32), axis=1).astype(BF16)
    combine_w = jnp.sum(jnp.where(matches, gates[:, :, None], F32(0.0)), axis=1)
    projected, gate_up_w = project(attn_out, w_proj, w_in.reshape(width_block, 2 * slice_units))
    outgoing = jnp.einsum(
        "tgc,td->gcd",
        dispatch_w.reshape(-1, groups, CAP),
        projected,
        preferred_element_type=F32,
    ).astype(BF16)
    down_w = w_out.reshape(slice_units, width_block)
    received = lax.all_to_all(outgoing, EXPERT, split_axis=0, concat_axis=0, tiled=True)
    flat_rows = received.reshape(groups * CAP, width_block)
    gate_up = jnp.dot(flat_rows, gate_up_w, preferred_element_type=F32).astype(BF16)
    quarter = groups * CAP // 4
    gate_up = lax.all_to_all(
        gate_up.reshape(4, quarter, 2 * slice_units), "tensor", split_axis=0, concat_axis=0, tiled=True
    )
    gate_up = jnp.sum(gate_up.astype(F32), axis=0)
    hidden = (jax.nn.silu(gate_up[:, :slice_units]) * gate_up[:, slice_units:]).astype(BF16)
    hidden = lax.all_to_all(
        jnp.broadcast_to(hidden[None], (4, quarter, slice_units)),
        "tensor",
        split_axis=0,
        concat_axis=0,
        tiled=True,
    ).reshape(groups * CAP, slice_units)
    result = jnp.dot(hidden, down_w, preferred_element_type=F32)
    returned = lax.all_to_all(
        result.reshape(groups, CAP, width_block).astype(BF16),
        EXPERT,
        split_axis=0,
        concat_axis=0,
        tiled=True,
    ).reshape(groups * CAP, width_block)
    moe_out = jnp.dot(
        combine_w, returned.astype(F32), precision=lax.Precision.HIGHEST, preferred_element_type=F32
    )
    return (projected, moe_out.astype(BF16))


def solution(mesh):
    split = Mesh(
        mesh.devices.reshape(2, 2, 4, 2, 4, 2, 4),
        ("plane", "core", "yh", "yl", "xh", "xl", "tensor"),
    )
    rows = ("plane", "core") + EXPERT
    placed = (
        P(rows, "tensor"),
        P("tensor", EXPERT),
        P(EXPERT, "tensor", None, None),
        P(EXPERT, None, "tensor"),
        P(rows, None),
        P(rows, None),
        P(rows, None),
    )
    return jax.shard_map(
        per_device,
        mesh=split,
        in_specs=placed,
        out_specs=(P(rows, "tensor"), P(rows, "tensor")),
        check_vma=False,
    )
```

```python
import jax
import jax.numpy as jnp
from jax import lax
from jax.experimental import pallas as pl
from jax.experimental.pallas import tpu as pltpu
from jax.sharding import Mesh, PartitionSpec as P

HSPLIT = 4
CAP = 2
EXPERT = ("yh", "yl", "xh", "xl")
NEAR = ("yl", "xh", "xl")
FAR = ("yh", "tensor")
BF16 = jnp.bfloat16
F32 = jnp.float32


VMEM = pl.BlockSpec(memory_space=pltpu.VMEM)
SMEM = pl.BlockSpec(memory_space=pltpu.SMEM)
ANY = pl.BlockSpec(memory_space=pl.ANY)


def address_kernel(attn_ref, sent_ref, staged, in_sems, out_sems):
    part = attn_ref.shape[1] // 4
    copies = []
    for m in range(4):
        for yh in range(4):
            at = m * 4 + yh
            copies.append(
                pltpu.make_async_copy(
                    attn_ref.at[:, pl.ds(m * part, part)], staged.at[at], in_sems.at[at]
                )
            )
    for copy in copies:
        copy.start()
    for copy in copies:
        copy.wait()
    copies = [
        pltpu.make_async_copy(
            staged.at[pl.ds(i // 4 * 8, 8)], sent_ref.at[pl.ds(i * 8, 8)], out_sems.at[i]
        )
        for i in range(8)
    ]
    for copy in copies:
        copy.start()
    for copy in copies:
        copy.wait()


def address(attn_out):
    rows, part = attn_out.shape[0], attn_out.shape[1] // 4
    return pl.pallas_call(
        address_kernel,
        out_shape=jax.ShapeDtypeStruct((64, rows, part), BF16),
        in_specs=[ANY],
        out_specs=ANY,
        scratch_shapes=[
            pltpu.VMEM((16, rows, part), BF16),
            pltpu.SemaphoreType.DMA((16,)),
            pltpu.SemaphoreType.DMA((8,)),
        ],
        compiler_params=pltpu.CompilerParams(vmem_limit_bytes=58 << 20),
        name="address",
    )(attn_out)


def cut_kernel(me, w_ref, *pieces):
    part = pieces[0].shape[1]
    for d in range(4):
        start = pl.multiple_of((me[0] ^ d) * part, part)
        pieces[d][...] = w_ref[:, pl.ds(start, part)]


def cut(me, w_cols):
    cols, part = w_cols.shape[0], w_cols.shape[1] // 4
    return pl.pallas_call(
        cut_kernel,
        out_shape=[jax.ShapeDtypeStruct((cols, part), BF16)] * 4,
        in_specs=[SMEM, VMEM],
        out_specs=[VMEM] * 4,
        compiler_params=pltpu.CompilerParams(vmem_limit_bytes=8 << 20),
        name="cut",
    )(me, w_cols)


def partial_kernel(me, tokens, *refs):
    blocks, (out_ref, wide) = refs[:4], refs[4:]
    cols = blocks[0].shape[0]
    for d in range(4):
        wide[pl.ds(pl.multiple_of((me[0] ^ d) * cols, 16), cols), :] = blocks[d][...]
    out_ref[...] = lax.dot_general(
        tokens[...], wide[...], (((1,), (1,)), ((), ())), preferred_element_type=F32
    ).astype(BF16)


def partial_sums(me, tokens, blocks):
    cols, part = blocks[0].shape
    return pl.pallas_call(
        partial_kernel,
        out_shape=jax.ShapeDtypeStruct((tokens.shape[0], 4 * cols), BF16),
        in_specs=[SMEM] + [VMEM] * 5,
        out_specs=VMEM,
        scratch_shapes=[pltpu.VMEM((4 * cols, part), BF16)],
        compiler_params=pltpu.CompilerParams(vmem_limit_bytes=16 << 20),
        name="partial_sums",
    )(me, tokens, *blocks)


def project(attn_out, w_proj, gate_up_w):
    rows, cols = attn_out.shape[0], w_proj.shape[1]
    me = lax.axis_index(("yl", "xl")).reshape(1).astype(jnp.int32)
    tokens = lax.all_to_all(address(attn_out), NEAR + ("yh",), split_axis=0, concat_axis=0, tiled=True)
    blocks = list(cut(me, w_proj.T))
    for d in range(1, 4):
        blocks[d] = lax.ppermute(blocks[d], ("yl", "xl"), [(i, i ^ d) for i in range(4)])
    tokens, gate_up_w = lax.optimization_barrier((tokens, gate_up_w))
    partial = partial_sums(me, tokens.reshape(64 * rows, -1), blocks)
    got = lax.all_to_all(
        partial.reshape(16, 4 * rows, 4 * cols), NEAR, split_axis=0, concat_axis=0, tiled=True
    )
    got = jnp.sum(got.reshape(2, 4, 2, 4 * rows, 4 * cols).astype(F32), axis=(0, 2))
    got = got.astype(BF16).reshape(4, 4, rows, 4 * cols).transpose(1, 0, 2, 3)
    real = jnp.arange(4, dtype=jnp.int32) == lax.axis_index("yh")
    got = jnp.where(real[None, :, None, None, None], got[:, None], BF16(0))
    got = lax.all_to_all(
        got.reshape(16, 4, rows, 4 * cols), FAR, split_axis=0, concat_axis=0, tiled=True
    )
    total = jnp.sum(got.astype(F32), axis=0).astype(BF16)
    total = total.reshape(4, rows, 2, 2, cols).transpose(1, 2, 0, 3, 4).reshape(rows, 16 * cols)
    return total, gate_up_w


def per_device(attn_out, w_proj, w_in, w_out, expert_ids, slots, gates):
    groups = lax.axis_size(EXPERT)
    width_block = w_in.shape[1]
    slice_units = w_in.shape[3]
    row = jnp.arange(groups * CAP, dtype=jnp.int32)
    matches = (expert_ids[:, :, None] == row // (HSPLIT * CAP)) & (slots[:, :, None] == row % CAP)
    dispatch_w = jnp.sum(matches.astype(F32), axis=1).astype(BF16)
    combine_w = jnp.sum(jnp.where(matches, gates[:, :, None], F32(0.0)), axis=1)
    projected, gate_up_w = project(attn_out, w_proj, w_in.reshape(width_block, 2 * slice_units))
    outgoing = jnp.einsum(
        "tgc,td->gcd",
        dispatch_w.reshape(-1, groups, CAP),
        projected,
        preferred_element_type=F32,
    ).astype(BF16)
    down_w = w_out.reshape(slice_units, width_block)
    received = lax.all_to_all(outgoing, EXPERT, split_axis=0, concat_axis=0, tiled=True)
    flat_rows = received.reshape(groups * CAP, width_block)
    gate_up = jnp.dot(flat_rows, gate_up_w, preferred_element_type=F32).astype(BF16)
    quarter = groups * CAP // 4
    gate_up = lax.all_to_all(
        gate_up.reshape(4, quarter, 2 * slice_units), "tensor", split_axis=0, concat_axis=0, tiled=True
    )
    gate_up = jnp.sum(gate_up.astype(F32), axis=0)
    hidden = (jax.nn.silu(gate_up[:, :slice_units]) * gate_up[:, slice_units:]).astype(BF16)
    hidden = lax.all_to_all(
        jnp.broadcast_to(hidden[None], (4, quarter, slice_units)),
        "tensor",
        split_axis=0,
        concat_axis=0,
        tiled=True,
    ).reshape(groups * CAP, slice_units)
    result = jnp.dot(hidden, down_w, preferred_element_type=F32)
    returned = lax.all_to_all(
        result.reshape(groups, CAP, width_block).astype(BF16),
        EXPERT,
        split_axis=0,
        concat_axis=0,
        tiled=True,
    ).reshape(groups * CAP, width_block)
    moe_out = jnp.dot(
        combine_w, returned.astype(F32), precision=lax.Precision.HIGHEST, preferred_element_type=F32
    )
    return (projected, moe_out.astype(BF16))


def solution(mesh):
    split = Mesh(
        mesh.devices.reshape(2, 2, 4, 2, 4, 2, 4),
        ("plane", "core", "yh", "yl", "xh", "xl", "tensor"),
    )
    rows = ("plane", "core") + EXPERT
    placed = (
        P(rows, "tensor"),
        P("tensor", EXPERT),
        P(EXPERT, "tensor", None, None),
        P(EXPERT, None, "tensor"),
        P(rows, None),
        P(rows, None),
        P(rows, None),
    )
    return jax.shard_map(
        per_device,
        mesh=split,
        in_specs=placed,
        out_specs=(P(rows, "tensor"), P(rows, "tensor")),
        check_vma=False,
    )
```

```python
import jax
import jax.numpy as jnp
from jax import lax
from jax.experimental import pallas as pl
from jax.experimental.pallas import tpu as pltpu
from jax.sharding import Mesh, PartitionSpec as P

HSPLIT = 4
CAP = 2
EXPERT = ("yh", "yl", "xh", "xl")
BF16 = jnp.bfloat16
F32 = jnp.float32


VMEM = pl.BlockSpec(memory_space=pltpu.VMEM)
SMEM = pl.BlockSpec(memory_space=pltpu.SMEM)
ANY = pl.BlockSpec(memory_space=pl.ANY)


def address_kernel(attn_ref, sent_ref, staged, in_sems, out_sems):
    part = attn_ref.shape[1] // 4
    copies = []
    for m in range(4):
        for x in range(4):
            at = (m // 2) * 8 + x * 2 + m % 2
            copies.append(
                pltpu.make_async_copy(
                    attn_ref.at[:, pl.ds(m * part, part)], staged.at[at], in_sems.at[at]
                )
            )
    for copy in copies:
        copy.start()
    for copy in copies:
        copy.wait()
    copies = [
        pltpu.make_async_copy(staged, sent_ref.at[pl.ds(yh * 16, 16)], out_sems.at[yh])
        for yh in range(4)
    ]
    for copy in copies:
        copy.start()
    for copy in copies:
        copy.wait()


def address(attn_out):
    rows, part = attn_out.shape[0], attn_out.shape[1] // 4
    return pl.pallas_call(
        address_kernel,
        out_shape=jax.ShapeDtypeStruct((64, rows, part), BF16),
        in_specs=[ANY],
        out_specs=ANY,
        scratch_shapes=[
            pltpu.VMEM((16, rows, part), BF16),
            pltpu.SemaphoreType.DMA((16,)),
            pltpu.SemaphoreType.DMA((4,)),
        ],
        compiler_params=pltpu.CompilerParams(vmem_limit_bytes=58 << 20),
        name="address",
    )(attn_out)


def cut_kernel(me, w_ref, *pieces):
    part = pieces[0].shape[1]
    for d in range(4):
        start = pl.multiple_of((me[0] ^ d) * part, part)
        pieces[d][...] = w_ref[:, pl.ds(start, part)]


def cut(me, w_cols):
    cols, part = w_cols.shape[0], w_cols.shape[1] // 4
    return pl.pallas_call(
        cut_kernel,
        out_shape=[jax.ShapeDtypeStruct((cols, part), BF16)] * 4,
        in_specs=[SMEM, VMEM],
        out_specs=[VMEM] * 4,
        compiler_params=pltpu.CompilerParams(vmem_limit_bytes=8 << 20),
        name="cut",
    )(me, w_cols)


def partial_kernel(me, tokens, *refs):
    blocks, (out_ref, wide) = refs[:4], refs[4:]
    cols = blocks[0].shape[0]
    spare = wide.shape[0] - 4 * cols
    wide[pl.ds(4 * cols, spare), :] = jnp.zeros((spare, wide.shape[1]), BF16)
    for d in range(4):
        wide[pl.ds(pl.multiple_of((me[0] ^ d) * cols, 16), cols), :] = blocks[d][...]
    out_ref[...] = lax.dot_general(
        tokens[...], wide[...], (((1,), (1,)), ((), ())), preferred_element_type=F32
    ).astype(BF16)


def partial_sums(me, tokens, blocks):
    cols, part = blocks[0].shape
    padded = -(-4 * cols // 128) * 128
    return pl.pallas_call(
        partial_kernel,
        out_shape=jax.ShapeDtypeStruct((tokens.shape[0], padded), BF16),
        in_specs=[SMEM] + [VMEM] * 5,
        out_specs=VMEM,
        scratch_shapes=[pltpu.VMEM((padded, part), BF16)],
        compiler_params=pltpu.CompilerParams(vmem_limit_bytes=16 << 20),
        name="partial_sums",
    )(me, tokens, *blocks)


def project(attn_out, w_proj, gate_up_w):
    rows, cols = attn_out.shape[0], w_proj.shape[1]
    me = lax.axis_index(("yl", "xl")).reshape(1).astype(jnp.int32)
    tokens = lax.all_to_all(address(attn_out), EXPERT, split_axis=0, concat_axis=0, tiled=True)
    blocks = list(cut(me, w_proj.T))
    for d in range(1, 4):
        blocks[d] = lax.ppermute(blocks[d], ("yl", "xl"), [(i, i ^ d) for i in range(4)])
    tokens, gate_up_w = lax.optimization_barrier((tokens, gate_up_w))
    partial = partial_sums(me, tokens.reshape(64 * rows, -1), blocks)
    got = lax.all_to_all(
        partial.reshape(64, rows, -1), EXPERT, split_axis=0, concat_axis=0, tiled=True
    )
    got = got.reshape(4, 2, 4, 2, rows, -1)[..., : 4 * cols].astype(F32)
    got = jnp.sum(got, axis=(1, 3)).astype(BF16)
    got = lax.all_to_all(got, "tensor", split_axis=0, concat_axis=0, tiled=True)
    total = jnp.sum(got.astype(F32), axis=0).astype(BF16)
    total = total.reshape(4, rows, 2, 2, cols).transpose(1, 2, 0, 3, 4).reshape(rows, 16 * cols)
    return total, gate_up_w


def per_device(attn_out, w_proj, w_in, w_out, expert_ids, slots, gates):
    groups = lax.axis_size(EXPERT)
    width_block = w_in.shape[1]
    slice_units = w_in.shape[3]
    row = jnp.arange(groups * CAP, dtype=jnp.int32)
    matches = (expert_ids[:, :, None] == row // (HSPLIT * CAP)) & (slots[:, :, None] == row % CAP)
    dispatch_w = jnp.sum(matches.astype(F32), axis=1).astype(BF16)
    combine_w = jnp.sum(jnp.where(matches, gates[:, :, None], F32(0.0)), axis=1)
    projected, gate_up_w = project(attn_out, w_proj, w_in.reshape(width_block, 2 * slice_units))
    outgoing = jnp.einsum(
        "tgc,td->gcd",
        dispatch_w.reshape(-1, groups, CAP),
        projected,
        preferred_element_type=F32,
    ).astype(BF16)
    down_w = w_out.reshape(slice_units, width_block)
    received = lax.all_to_all(outgoing, EXPERT, split_axis=0, concat_axis=0, tiled=True)
    flat_rows = received.reshape(groups * CAP, width_block)
    gate_up = jnp.dot(flat_rows, gate_up_w, preferred_element_type=F32).astype(BF16)
    quarter = groups * CAP // 4
    gate_up = lax.all_to_all(
        gate_up.reshape(4, quarter, 2 * slice_units), "tensor", split_axis=0, concat_axis=0, tiled=True
    )
    gate_up = jnp.sum(gate_up.astype(F32), axis=0)
    hidden = (jax.nn.silu(gate_up[:, :slice_units]) * gate_up[:, slice_units:]).astype(BF16)
    hidden = lax.all_to_all(
        jnp.broadcast_to(hidden[None], (4, quarter, slice_units)),
        "tensor",
        split_axis=0,
        concat_axis=0,
        tiled=True,
    ).reshape(groups * CAP, slice_units)
    result = jnp.dot(hidden, down_w, preferred_element_type=F32)
    returned = lax.all_to_all(
        result.reshape(groups, CAP, width_block).astype(BF16),
        EXPERT,
        split_axis=0,
        concat_axis=0,
        tiled=True,
    ).reshape(groups * CAP, width_block)
    moe_out = jnp.dot(
        combine_w, returned.astype(F32), precision=lax.Precision.HIGHEST, preferred_element_type=F32
    )
    return (projected, moe_out.astype(BF16))


def solution(mesh):
    split = Mesh(
        mesh.devices.reshape(2, 2, 4, 2, 4, 2, 4),
        ("plane", "core", "yh", "yl", "xh", "xl", "tensor"),
    )
    rows = ("plane", "core") + EXPERT
    placed = (
        P(rows, "tensor"),
        P("tensor", EXPERT),
        P(EXPERT, "tensor", None, None),
        P(EXPERT, None, "tensor"),
        P(rows, None),
        P(rows, None),
        P(rows, None),
    )
    return jax.shard_map(
        per_device,
        mesh=split,
        in_specs=placed,
        out_specs=(P(rows, "tensor"), P(rows, "tensor")),
        check_vma=False,
    )
```

```python
import jax
import jax.numpy as jnp
from jax import lax
from jax.experimental import pallas as pl
from jax.experimental.pallas import tpu as pltpu
from jax.sharding import Mesh, PartitionSpec as P

HSPLIT = 4
CAP = 2
EXPERT = ("yh", "yl", "xh", "xl")
BF16 = jnp.bfloat16
F32 = jnp.float32


VMEM = pl.BlockSpec(memory_space=pltpu.VMEM)
SMEM = pl.BlockSpec(memory_space=pltpu.SMEM)
ANY = pl.BlockSpec(memory_space=pl.ANY)


def address_kernel(attn_ref, sent_ref, staged, in_sems, out_sems):
    part = attn_ref.shape[1] // 4
    copies = []
    for m in range(4):
        for x in range(4):
            at = (m // 2) * 8 + x * 2 + m % 2
            copies.append(
                pltpu.make_async_copy(
                    attn_ref.at[:, pl.ds(m * part, part)], staged.at[at], in_sems.at[at]
                )
            )
    for copy in copies:
        copy.start()
    for copy in copies:
        copy.wait()
    copies = [
        pltpu.make_async_copy(staged, sent_ref.at[pl.ds(yh * 16, 16)], out_sems.at[yh])
        for yh in range(4)
    ]
    for copy in copies:
        copy.start()
    for copy in copies:
        copy.wait()


def address(attn_out):
    rows, part = attn_out.shape[0], attn_out.shape[1] // 4
    return pl.pallas_call(
        address_kernel,
        out_shape=jax.ShapeDtypeStruct((64, rows, part), BF16),
        in_specs=[ANY],
        out_specs=ANY,
        scratch_shapes=[
            pltpu.VMEM((16, rows, part), BF16),
            pltpu.SemaphoreType.DMA((16,)),
            pltpu.SemaphoreType.DMA((4,)),
        ],
        compiler_params=pltpu.CompilerParams(vmem_limit_bytes=58 << 20),
        name="address",
    )(attn_out)


def cut_kernel(me, w_ref, *pieces):
    part = pieces[0].shape[1]
    for d in range(4):
        start = pl.multiple_of((me[0] ^ d) * part, part)
        pieces[d][...] = w_ref[:, pl.ds(start, part)]


def cut(me, w_cols):
    cols, part = w_cols.shape[0], w_cols.shape[1] // 4
    return pl.pallas_call(
        cut_kernel,
        out_shape=[jax.ShapeDtypeStruct((cols, part), BF16)] * 4,
        in_specs=[SMEM, VMEM],
        out_specs=[VMEM] * 4,
        compiler_params=pltpu.CompilerParams(vmem_limit_bytes=8 << 20),
        name="cut",
    )(me, w_cols)


def partial_kernel(me, tokens, *refs):
    blocks, (out_ref, wide) = refs[:4], refs[4:]
    cols = blocks[0].shape[0]
    spare = wide.shape[0] - 4 * cols
    wide[pl.ds(4 * cols, spare), :] = jnp.zeros((spare, wide.shape[1]), BF16)
    for d in range(4):
        wide[pl.ds(pl.multiple_of((me[0] ^ d) * cols, 16), cols), :] = blocks[d][...]
    out_ref[...] = lax.dot_general(
        tokens[...], wide[...], (((1,), (1,)), ((), ())), preferred_element_type=F32
    ).astype(BF16)


def partial_sums(me, tokens, blocks):
    cols, part = blocks[0].shape
    padded = -(-4 * cols // 128) * 128
    return pl.pallas_call(
        partial_kernel,
        out_shape=jax.ShapeDtypeStruct((tokens.shape[0], padded), BF16),
        in_specs=[SMEM] + [VMEM] * 5,
        out_specs=VMEM,
        scratch_shapes=[pltpu.VMEM((padded, part), BF16)],
        compiler_params=pltpu.CompilerParams(vmem_limit_bytes=16 << 20),
        name="partial_sums",
    )(me, tokens, *blocks)


CHIPS = ("core",) + EXPERT
PLACES = [
    [64 * core + (y + core) % 8 * 8 + (x + core) % 8 for y in range(8) for x in range(8)]
    for core in range(2)
]


def trade(block, d):
    flip = (d // 2) * 8 + d % 2
    pairs = [(places[p], places[p ^ flip]) for places in PLACES for p in range(64)]
    return lax.ppermute(block, CHIPS, pairs)


def spread(pieces):
    return lax.all_to_all(
        pieces, CHIPS, split_axis=0, concat_axis=0, tiled=True, axis_index_groups=PLACES
    )


def project(attn_out, w_proj, gate_up_w):
    rows, cols = attn_out.shape[0], w_proj.shape[1]
    core = lax.axis_index("core")
    me = (lax.axis_index(("yl", "xl")) ^ (core * 3)).reshape(1).astype(jnp.int32)
    tokens = spread(address(attn_out))
    blocks = list(cut(me, w_proj.T))
    for d in range(1, 4):
        blocks[d] = trade(blocks[d], d)
    lane = jnp.arange(4 * cols, dtype=jnp.int32)
    moves = jnp.broadcast_to((lane >= 2 * cols) & (core == 1), (rows, 4 * cols))
    tokens, gate_up_w, moves = lax.optimization_barrier((tokens, gate_up_w, moves))
    partial = partial_sums(me, tokens.reshape(64 * rows, -1), blocks)
    got = spread(partial.reshape(64, rows, -1))
    got = got.reshape(4, 2, 4, 2, rows, -1)[..., : 4 * cols].astype(F32)
    got = jnp.sum(got, axis=(1, 3)).astype(BF16)
    got = jnp.where(moves, jnp.roll(got, 1, axis=0), got)
    got = lax.all_to_all(got, "tensor", split_axis=0, concat_axis=0, tiled=True)
    total = jnp.sum(got.astype(F32), axis=0).astype(BF16)
    total = total.reshape(4, rows, 2, 2, cols).transpose(1, 2, 0, 3, 4).reshape(rows, 2, 8, cols)
    total = jnp.where(core == 1, jnp.roll(total[:, ::-1], 1, axis=2), total)
    return total.reshape(rows, 16 * cols), gate_up_w


def per_device(attn_out, w_proj, w_in, w_out, expert_ids, slots, gates):
    groups = lax.axis_size(EXPERT)
    width_block = w_in.shape[1]
    slice_units = w_in.shape[3]
    row = jnp.arange(groups * CAP, dtype=jnp.int32)
    matches = (expert_ids[:, :, None] == row // (HSPLIT * CAP)) & (slots[:, :, None] == row % CAP)
    dispatch_w = jnp.sum(matches.astype(F32), axis=1).astype(BF16)
    combine_w = jnp.sum(jnp.where(matches, gates[:, :, None], F32(0.0)), axis=1)
    projected, gate_up_w = project(attn_out, w_proj, w_in.reshape(width_block, 2 * slice_units))
    outgoing = jnp.einsum(
        "tgc,td->gcd",
        dispatch_w.reshape(-1, groups, CAP),
        projected,
        preferred_element_type=F32,
    ).astype(BF16)
    down_w = w_out.reshape(slice_units, width_block)
    received = lax.all_to_all(outgoing, EXPERT, split_axis=0, concat_axis=0, tiled=True)
    flat_rows = received.reshape(groups * CAP, width_block)
    gate_up = jnp.dot(flat_rows, gate_up_w, preferred_element_type=F32).astype(BF16)
    quarter = groups * CAP // 4
    gate_up = lax.all_to_all(
        gate_up.reshape(4, quarter, 2 * slice_units), "tensor", split_axis=0, concat_axis=0, tiled=True
    )
    gate_up = jnp.sum(gate_up.astype(F32), axis=0)
    hidden = (jax.nn.silu(gate_up[:, :slice_units]) * gate_up[:, slice_units:]).astype(BF16)
    hidden = lax.all_to_all(
        jnp.broadcast_to(hidden[None], (4, quarter, slice_units)),
        "tensor",
        split_axis=0,
        concat_axis=0,
        tiled=True,
    ).reshape(groups * CAP, slice_units)
    result = jnp.dot(hidden, down_w, preferred_element_type=F32)
    returned = lax.all_to_all(
        result.reshape(groups, CAP, width_block).astype(BF16),
        EXPERT,
        split_axis=0,
        concat_axis=0,
        tiled=True,
    ).reshape(groups * CAP, width_block)
    moe_out = jnp.dot(
        combine_w, returned.astype(F32), precision=lax.Precision.HIGHEST, preferred_element_type=F32
    )
    return (projected, moe_out.astype(BF16))


def solution(mesh):
    split = Mesh(
        mesh.devices.reshape(2, 2, 4, 2, 4, 2, 4),
        ("plane", "core", "yh", "yl", "xh", "xl", "tensor"),
    )
    rows = ("plane", "core") + EXPERT
    placed = (
        P(rows, "tensor"),
        P("tensor", EXPERT),
        P(EXPERT, "tensor", None, None),
        P(EXPERT, None, "tensor"),
        P(rows, None),
        P(rows, None),
        P(rows, None),
    )
    return jax.shard_map(
        per_device,
        mesh=split,
        in_specs=placed,
        out_specs=(P(rows, "tensor"), P(rows, "tensor")),
        check_vma=False,
    )
```

```python
import jax
import jax.numpy as jnp
from jax import lax
from jax.experimental import pallas as pl
from jax.experimental.pallas import tpu as pltpu
from jax.sharding import Mesh, PartitionSpec as P

HSPLIT = 4
CAP = 2
EXPERT = ("yh", "yl", "xh", "xl")
BF16 = jnp.bfloat16
F32 = jnp.float32


VMEM = pl.BlockSpec(memory_space=pltpu.VMEM)
SMEM = pl.BlockSpec(memory_space=pltpu.SMEM)
ANY = pl.BlockSpec(memory_space=pl.ANY)


def prepare_kernel(me, attn_ref, w_ref, sent_ref, *refs):
    pieces, (staged, w_held, in_sems, out_sems) = refs[:4], refs[4:]
    part = attn_ref.shape[1] // 4
    arrivals = []
    for m in range(4):
        for x in range(4):
            at = (m // 2) * 8 + x * 2 + m % 2
            arrivals.append(
                pltpu.make_async_copy(
                    attn_ref.at[:, pl.ds(m * part, part)], staged.at[at], in_sems.at[at]
                )
            )
    weights = pltpu.make_async_copy(w_ref, w_held, in_sems.at[16])
    for copy in arrivals:
        copy.start()
    weights.start()
    for copy in arrivals:
        copy.wait()
    leaving = [
        pltpu.make_async_copy(staged, sent_ref.at[pl.ds(yh * 16, 16)], out_sems.at[yh])
        for yh in range(4)
    ]
    for copy in leaving:
        copy.start()
    weights.wait()
    for d in range(4):
        start = pl.multiple_of((me[0] ^ d) * part, part)
        leaving.append(
            pltpu.make_async_copy(w_held.at[:, pl.ds(start, part)], pieces[d], out_sems.at[4 + d])
        )
        leaving[-1].start()
    for copy in leaving:
        copy.wait()


def prepare(me, attn_out, w_cols):
    rows, cols = attn_out.shape[0], w_cols.shape[0]
    part = attn_out.shape[1] // 4
    return pl.pallas_call(
        prepare_kernel,
        out_shape=[jax.ShapeDtypeStruct((64, rows, part), BF16)]
        + [jax.ShapeDtypeStruct((cols, part), BF16)] * 4,
        in_specs=[SMEM, ANY, ANY],
        out_specs=[ANY] * 5,
        scratch_shapes=[
            pltpu.VMEM((16, rows, part), BF16),
            pltpu.VMEM(w_cols.shape, BF16),
            pltpu.SemaphoreType.DMA((17,)),
            pltpu.SemaphoreType.DMA((8,)),
        ],
        compiler_params=pltpu.CompilerParams(vmem_limit_bytes=58 << 20),
        name="prepare",
    )(me, attn_out, w_cols)


def gate_up_kernel(routed, weights, out_ref):
    out_ref[...] = jnp.dot(routed[...], weights[...], preferred_element_type=F32).astype(BF16)


def gate_up_product(routed, weights):
    return pl.pallas_call(
        gate_up_kernel,
        out_shape=jax.ShapeDtypeStruct((routed.shape[0], weights.shape[1]), BF16),
        in_specs=[VMEM] * 2,
        out_specs=VMEM,
        compiler_params=pltpu.CompilerParams(vmem_limit_bytes=16 << 20),
        name="gate_up_product",
    )(routed, weights)


def partial_kernel(me, tokens, *refs):
    blocks, (out_ref, wide) = refs[:4], refs[4:]
    cols = blocks[0].shape[0]
    spare = wide.shape[0] - 4 * cols
    wide[pl.ds(4 * cols, spare), :] = jnp.zeros((spare, wide.shape[1]), BF16)
    for d in range(4):
        wide[pl.ds(pl.multiple_of((me[0] ^ d) * cols, 16), cols), :] = blocks[d][...]
    out_ref[...] = lax.dot_general(
        tokens[...], wide[...], (((1,), (1,)), ((), ())), preferred_element_type=F32
    ).astype(BF16)


def partial_sums(me, tokens, blocks):
    cols, part = blocks[0].shape
    padded = -(-4 * cols // 128) * 128
    return pl.pallas_call(
        partial_kernel,
        out_shape=jax.ShapeDtypeStruct((tokens.shape[0], padded), BF16),
        in_specs=[SMEM] + [VMEM] * 5,
        out_specs=VMEM,
        scratch_shapes=[pltpu.VMEM((padded, part), BF16)],
        compiler_params=pltpu.CompilerParams(vmem_limit_bytes=16 << 20),
        name="partial_sums",
    )(me, tokens, *blocks)


CHIPS = ("core",) + EXPERT
PLACES = [
    [64 * core + (y + core) % 8 * 8 + (x + core) % 8 for y in range(8) for x in range(8)]
    for core in range(2)
]


def trade(block, d):
    flip = (d // 2) * 8 + d % 2
    pairs = [(places[p], places[p ^ flip]) for places in PLACES for p in range(64)]
    return lax.ppermute(block, CHIPS, pairs)


def spread(pieces):
    return lax.all_to_all(
        pieces, CHIPS, split_axis=0, concat_axis=0, tiled=True, axis_index_groups=PLACES
    )


def project(attn_out, w_proj, gate_up_w):
    rows, cols = attn_out.shape[0], w_proj.shape[1]
    core = lax.axis_index("core")
    me = (lax.axis_index(("yl", "xl")) ^ (core * 3)).reshape(1).astype(jnp.int32)
    sent, *blocks = prepare(me, attn_out, w_proj.T)
    tokens = spread(sent)
    for d in range(1, 4):
        blocks[d] = trade(blocks[d], d)
    lane = jnp.arange(4 * cols, dtype=jnp.int32)
    moves = jnp.broadcast_to((lane >= 2 * cols) & (core == 1), (rows, 4 * cols))
    tokens, gate_up_w, moves = lax.optimization_barrier((tokens, gate_up_w, moves))
    partial = partial_sums(me, tokens.reshape(64 * rows, -1), blocks)
    got = spread(partial.reshape(64, rows, -1))
    got = got.reshape(4, 2, 4, 2, rows, -1)[..., : 4 * cols].astype(F32)
    got = jnp.sum(got, axis=(1, 3)).astype(BF16)
    got = jnp.where(moves, jnp.roll(got, 1, axis=0), got)
    got = lax.all_to_all(got, "tensor", split_axis=0, concat_axis=0, tiled=True)
    total = jnp.sum(got.astype(F32), axis=0).astype(BF16)
    total = total.reshape(4, rows, 2, 2, cols).transpose(1, 2, 0, 3, 4).reshape(rows, 2, 8, cols)
    total = jnp.where(core == 1, jnp.roll(total[:, ::-1], 1, axis=2), total)
    return total.reshape(rows, 16 * cols), gate_up_w


def per_device(attn_out, w_proj, w_in, w_out, expert_ids, slots, gates):
    groups = lax.axis_size(EXPERT)
    width_block = w_in.shape[1]
    slice_units = w_in.shape[3]
    row = jnp.arange(groups * CAP, dtype=jnp.int32)
    matches = (expert_ids[:, :, None] == row // (HSPLIT * CAP)) & (slots[:, :, None] == row % CAP)
    dispatch_w = jnp.sum(matches.astype(F32), axis=1).astype(BF16)
    combine_w = jnp.sum(jnp.where(matches, gates[:, :, None], F32(0.0)), axis=1)
    projected, gate_up_w = project(attn_out, w_proj, w_in.reshape(width_block, 2 * slice_units))
    outgoing = jnp.einsum(
        "tgc,td->gcd",
        dispatch_w.reshape(-1, groups, CAP),
        projected,
        preferred_element_type=F32,
    ).astype(BF16)
    down_w = w_out.reshape(slice_units, width_block)
    received = lax.all_to_all(outgoing, EXPERT, split_axis=0, concat_axis=0, tiled=True)
    flat_rows = received.reshape(groups * CAP, width_block)
    gate_up = gate_up_product(flat_rows, gate_up_w)
    quarter = groups * CAP // 4
    gate_up = lax.all_to_all(
        gate_up.reshape(4, quarter, 2 * slice_units), "tensor", split_axis=0, concat_axis=0, tiled=True
    )
    gate_up = jnp.sum(gate_up.astype(F32), axis=0)
    hidden = (jax.nn.silu(gate_up[:, :slice_units]) * gate_up[:, slice_units:]).astype(BF16)
    hidden = lax.all_to_all(
        jnp.broadcast_to(hidden[None], (4, quarter, slice_units)),
        "tensor",
        split_axis=0,
        concat_axis=0,
        tiled=True,
    ).reshape(groups * CAP, slice_units)
    result = jnp.dot(hidden, down_w, preferred_element_type=F32)
    returned = lax.all_to_all(
        result.reshape(groups, CAP, width_block).astype(BF16),
        EXPERT,
        split_axis=0,
        concat_axis=0,
        tiled=True,
    ).reshape(groups * CAP, width_block)
    moe_out = jnp.dot(
        combine_w, returned.astype(F32), precision=lax.Precision.HIGHEST, preferred_element_type=F32
    )
    return (projected, moe_out.astype(BF16))


def solution(mesh):
    split = Mesh(
        mesh.devices.reshape(2, 2, 4, 2, 4, 2, 4),
        ("plane", "core", "yh", "yl", "xh", "xl", "tensor"),
    )
    rows = ("plane", "core") + EXPERT
    placed = (
        P(rows, "tensor"),
        P("tensor", EXPERT),
        P(EXPERT, "tensor", None, None),
        P(EXPERT, None, "tensor"),
        P(rows, None),
        P(rows, None),
        P(rows, None),
    )
    return jax.shard_map(
        per_device,
        mesh=split,
        in_specs=placed,
        out_specs=(P(rows, "tensor"), P(rows, "tensor")),
        check_vma=False,
    )
```

```python
import jax
import jax.numpy as jnp
from jax import lax
from jax.experimental import pallas as pl
from jax.experimental.pallas import tpu as pltpu
from jax.sharding import Mesh, PartitionSpec as P

HSPLIT = 4
CAP = 2
EXPERT = ("yh", "yl", "xh", "xl")
BF16 = jnp.bfloat16
F32 = jnp.float32


VMEM = pl.BlockSpec(memory_space=pltpu.VMEM)
SMEM = pl.BlockSpec(memory_space=pltpu.SMEM)
ANY = pl.BlockSpec(memory_space=pl.ANY)


def address_kernel(attn_ref, sent_ref, staged, in_sems, out_sems):
    part = attn_ref.shape[1] // 4
    copies = []
    for m in range(4):
        for x in range(4):
            at = (m // 2) * 8 + x * 2 + m % 2
            copies.append(
                pltpu.make_async_copy(
                    attn_ref.at[:, pl.ds(m * part, part)], staged.at[at], in_sems.at[at]
                )
            )
    for copy in copies:
        copy.start()
    for copy in copies:
        copy.wait()
    copies = [
        pltpu.make_async_copy(staged, sent_ref.at[pl.ds(yh * 16, 16)], out_sems.at[yh])
        for yh in range(4)
    ]
    for copy in copies:
        copy.start()
    for copy in copies:
        copy.wait()


def address(attn_out):
    rows, part = attn_out.shape[0], attn_out.shape[1] // 4
    return pl.pallas_call(
        address_kernel,
        out_shape=jax.ShapeDtypeStruct((64, rows, part), BF16),
        in_specs=[ANY],
        out_specs=ANY,
        scratch_shapes=[
            pltpu.VMEM((16, rows, part), BF16),
            pltpu.SemaphoreType.DMA((16,)),
            pltpu.SemaphoreType.DMA((4,)),
        ],
        compiler_params=pltpu.CompilerParams(vmem_limit_bytes=58 << 20),
        name="address",
    )(attn_out)


def cut_kernel(me, w_ref, *pieces):
    part = pieces[0].shape[1]
    for d in range(4):
        start = pl.multiple_of((me[0] ^ d) * part, part)
        pieces[d][...] = w_ref[:, pl.ds(start, part)]


def cut(me, w_cols):
    cols, part = w_cols.shape[0], w_cols.shape[1] // 4
    return pl.pallas_call(
        cut_kernel,
        out_shape=[jax.ShapeDtypeStruct((cols, part), BF16)] * 4,
        in_specs=[SMEM, VMEM],
        out_specs=[VMEM] * 4,
        compiler_params=pltpu.CompilerParams(vmem_limit_bytes=8 << 20),
        name="cut",
    )(me, w_cols)


def partial_kernel(me, tokens, *refs):
    blocks, (out_ref, wide) = refs[:4], refs[4:]
    cols = blocks[0].shape[0]
    spare = wide.shape[0] - 4 * cols
    wide[pl.ds(4 * cols, spare), :] = jnp.zeros((spare, wide.shape[1]), BF16)
    for d in range(4):
        wide[pl.ds(pl.multiple_of((me[0] ^ d) * cols, 16), cols), :] = blocks[d][...]
    out_ref[...] = lax.dot_general(
        tokens[...], wide[...], (((1,), (1,)), ((), ())), preferred_element_type=F32
    ).astype(BF16)


def partial_sums(me, tokens, blocks):
    cols, part = blocks[0].shape
    padded = -(-4 * cols // 128) * 128
    return pl.pallas_call(
        partial_kernel,
        out_shape=jax.ShapeDtypeStruct((tokens.shape[0], padded), BF16),
        in_specs=[SMEM] + [VMEM] * 5,
        out_specs=VMEM,
        scratch_shapes=[pltpu.VMEM((padded, part), BF16)],
        compiler_params=pltpu.CompilerParams(vmem_limit_bytes=16 << 20),
        name="partial_sums",
    )(me, tokens, *blocks)


CHIPS = ("core",) + EXPERT
PLACES = [
    [64 * core + (y + core) % 8 * 8 + (x + core) % 8 for y in range(8) for x in range(8)]
    for core in range(2)
]


def trade(block, d):
    flip = (d // 2) * 8 + d % 2
    pairs = [(places[p], places[p ^ flip]) for places in PLACES for p in range(64)]
    return lax.ppermute(block, CHIPS, pairs)


def spread(pieces):
    return lax.all_to_all(
        pieces, CHIPS, split_axis=0, concat_axis=0, tiled=True, axis_index_groups=PLACES
    )


def project(attn_out, w_proj, beside):
    rows, cols = attn_out.shape[0], w_proj.shape[1]
    core = lax.axis_index("core")
    me = (lax.axis_index(("yl", "xl")) ^ (core * 3)).reshape(1).astype(jnp.int32)
    tokens = spread(address(attn_out))
    blocks = list(cut(me, w_proj.T))
    for d in range(1, 4):
        blocks[d] = trade(blocks[d], d)
    lane = jnp.arange(4 * cols, dtype=jnp.int32)
    moves = jnp.broadcast_to((lane >= 2 * cols) & (core == 1), (rows, 4 * cols))
    tokens, beside, moves = lax.optimization_barrier((tokens, beside, moves))
    partial = partial_sums(me, tokens.reshape(64 * rows, -1), blocks)
    got = spread(partial.reshape(64, rows, -1))
    got = got.reshape(4, 2, 4, 2, rows, -1)[..., : 4 * cols].astype(F32)
    got = jnp.sum(got, axis=(1, 3)).astype(BF16)
    got = jnp.where(moves, jnp.roll(got, 1, axis=0), got)
    got = lax.all_to_all(got, "tensor", split_axis=0, concat_axis=0, tiled=True)
    total = jnp.sum(got.astype(F32), axis=0).astype(BF16)
    total = total.reshape(4, rows, 2, 2, cols).transpose(1, 2, 0, 3, 4).reshape(rows, 2, 8, cols)
    total = jnp.where(core == 1, jnp.roll(total[:, ::-1], 1, axis=2), total)
    return lax.optimization_barrier(total.reshape(rows, 16 * cols)), beside


def per_device(attn_out, w_proj, w_in, w_out, expert_ids, slots, gates):
    groups = lax.axis_size(EXPERT)
    width_block = w_in.shape[1]
    slice_units = w_in.shape[3]
    row = jnp.arange(groups * CAP, dtype=jnp.int32)
    matches = (expert_ids[:, :, None] == row // (HSPLIT * CAP)) & (slots[:, :, None] == row % CAP)
    dispatch_w = jnp.sum(matches.astype(F32), axis=1).astype(BF16)
    combine_w = jnp.sum(jnp.where(matches, gates[:, :, None], F32(0.0)), axis=1)
    beside = (w_in.reshape(width_block, 2 * slice_units), dispatch_w.T, combine_w)
    projected, (gate_up_w, dispatch_w, combine_w) = project(attn_out, w_proj, beside)
    outgoing = jnp.einsum(
        "gct,td->gcd",
        dispatch_w.reshape(groups, CAP, -1),
        projected,
        preferred_element_type=F32,
    ).astype(BF16)
    down_w = w_out.reshape(slice_units, width_block)
    projected, outgoing = lax.optimization_barrier((projected, outgoing))
    received = lax.all_to_all(outgoing, EXPERT, split_axis=0, concat_axis=0, tiled=True)
    flat_rows = received.reshape(groups * CAP, width_block)
    gate_up = jnp.dot(flat_rows, gate_up_w, preferred_element_type=F32).astype(BF16)
    quarter = groups * CAP // 4
    gate_up = lax.all_to_all(
        gate_up.reshape(4, quarter, 2 * slice_units), "tensor", split_axis=0, concat_axis=0, tiled=True
    )
    gate_up = jnp.sum(gate_up.astype(F32), axis=0)
    hidden = (jax.nn.silu(gate_up[:, :slice_units]) * gate_up[:, slice_units:]).astype(BF16)
    hidden = lax.all_to_all(
        jnp.broadcast_to(hidden[None], (4, quarter, slice_units)),
        "tensor",
        split_axis=0,
        concat_axis=0,
        tiled=True,
    ).reshape(groups * CAP, slice_units)
    result = jnp.dot(hidden, down_w, preferred_element_type=F32)
    returned = lax.all_to_all(
        result.reshape(groups, CAP, width_block).astype(BF16),
        EXPERT,
        split_axis=0,
        concat_axis=0,
        tiled=True,
    ).reshape(groups * CAP, width_block)
    moe_out = jnp.dot(
        combine_w, returned.astype(F32), precision=lax.Precision.HIGHEST, preferred_element_type=F32
    )
    return (projected, moe_out.astype(BF16))


def solution(mesh):
    split = Mesh(
        mesh.devices.reshape(2, 2, 4, 2, 4, 2, 4),
        ("plane", "core", "yh", "yl", "xh", "xl", "tensor"),
    )
    rows = ("plane", "core") + EXPERT
    placed = (
        P(rows, "tensor"),
        P("tensor", EXPERT),
        P(EXPERT, "tensor", None, None),
        P(EXPERT, None, "tensor"),
        P(rows, None),
        P(rows, None),
        P(rows, None),
    )
    return jax.shard_map(
        per_device,
        mesh=split,
        in_specs=placed,
        out_specs=(P(rows, "tensor"), P(rows, "tensor")),
        check_vma=False,
    )
```

```python
import jax
import jax.numpy as jnp
from jax import lax
from jax.experimental import pallas as pl
from jax.experimental.pallas import tpu as pltpu
from jax.sharding import Mesh, PartitionSpec as P

HSPLIT = 4
CAP = 2
EXPERT = ("yh", "yl", "xh", "xl")
BF16 = jnp.bfloat16
F32 = jnp.float32


VMEM = pl.BlockSpec(memory_space=pltpu.VMEM)
SMEM = pl.BlockSpec(memory_space=pltpu.SMEM)
ANY = pl.BlockSpec(memory_space=pl.ANY)


def prepare_kernel(me, attn_ref, w_ref, sent_ref, *refs):
    pieces, (staged, w_held, in_sems, out_sems) = refs[:4], refs[4:]
    part = attn_ref.shape[1] // 4
    arrivals = []
    for m in range(4):
        for x in range(4):
            at = (m // 2) * 8 + x * 2 + m % 2
            arrivals.append(
                pltpu.make_async_copy(
                    attn_ref.at[:, pl.ds(m * part, part)], staged.at[at], in_sems.at[at]
                )
            )
    weights = pltpu.make_async_copy(w_ref, w_held, in_sems.at[16])
    for copy in arrivals:
        copy.start()
    weights.start()
    for copy in arrivals:
        copy.wait()
    leaving = [
        pltpu.make_async_copy(staged, sent_ref.at[pl.ds(yh * 16, 16)], out_sems.at[yh])
        for yh in range(4)
    ]
    for copy in leaving:
        copy.start()
    weights.wait()
    for d in range(4):
        start = pl.multiple_of((me[0] ^ d) * part, part)
        leaving.append(
            pltpu.make_async_copy(w_held.at[:, pl.ds(start, part)], pieces[d], out_sems.at[4 + d])
        )
        leaving[-1].start()
    for copy in leaving:
        copy.wait()


def prepare(me, attn_out, w_cols):
    rows, cols = attn_out.shape[0], w_cols.shape[0]
    part = attn_out.shape[1] // 4
    return pl.pallas_call(
        prepare_kernel,
        out_shape=[jax.ShapeDtypeStruct((64, rows, part), BF16)]
        + [jax.ShapeDtypeStruct((cols, part), BF16)] * 4,
        in_specs=[SMEM, ANY, ANY],
        out_specs=[ANY] * 5,
        scratch_shapes=[
            pltpu.VMEM((16, rows, part), BF16),
            pltpu.VMEM(w_cols.shape, BF16),
            pltpu.SemaphoreType.DMA((17,)),
            pltpu.SemaphoreType.DMA((8,)),
        ],
        compiler_params=pltpu.CompilerParams(vmem_limit_bytes=58 << 20),
        name="prepare",
    )(me, attn_out, w_cols)


def gate_up_kernel(routed, weights, out_ref, total):
    step = pl.program_id(0)
    depth = weights.shape[0]
    columns = pl.ds(pl.multiple_of(step * depth, depth), depth)

    @pl.when(step == 0)
    def _():
        total[...] = jnp.zeros_like(total)

    total[...] += jnp.dot(routed[:, columns], weights[...], preferred_element_type=F32)

    @pl.when(step == pl.num_programs(0) - 1)
    def _():
        out_ref[...] = total[...].astype(BF16)


def gate_up_product(routed, weights):
    rows, depth = routed.shape
    units, steps = weights.shape[1], 7
    return pl.pallas_call(
        gate_up_kernel,
        grid=(steps,),
        out_shape=jax.ShapeDtypeStruct((rows, units), BF16),
        in_specs=[VMEM, pl.BlockSpec((depth // steps, units), lambda k: (k, 0))],
        out_specs=VMEM,
        scratch_shapes=[pltpu.VMEM((rows, units), F32)],
        compiler_params=pltpu.CompilerParams(vmem_limit_bytes=58 << 20),
        name="gate_up_product",
    )(routed, weights)


def partial_kernel(me, tokens, *refs):
    blocks, (out_ref, wide) = refs[:4], refs[4:]
    cols = blocks[0].shape[0]
    spare = wide.shape[0] - 4 * cols
    wide[pl.ds(4 * cols, spare), :] = jnp.zeros((spare, wide.shape[1]), BF16)
    for d in range(4):
        wide[pl.ds(pl.multiple_of((me[0] ^ d) * cols, 16), cols), :] = blocks[d][...]
    out_ref[...] = lax.dot_general(
        tokens[...], wide[...], (((1,), (1,)), ((), ())), preferred_element_type=F32
    ).astype(BF16)


def partial_sums(me, tokens, blocks):
    cols, part = blocks[0].shape
    padded = -(-4 * cols // 128) * 128
    return pl.pallas_call(
        partial_kernel,
        out_shape=jax.ShapeDtypeStruct((tokens.shape[0], padded), BF16),
        in_specs=[SMEM] + [VMEM] * 5,
        out_specs=VMEM,
        scratch_shapes=[pltpu.VMEM((padded, part), BF16)],
        compiler_params=pltpu.CompilerParams(vmem_limit_bytes=16 << 20),
        name="partial_sums",
    )(me, tokens, *blocks)


CHIPS = ("core",) + EXPERT
PLACES = [
    [64 * core + (y + core) % 8 * 8 + (x + core) % 8 for y in range(8) for x in range(8)]
    for core in range(2)
]


def trade(block, d):
    flip = (d // 2) * 8 + d % 2
    pairs = [(places[p], places[p ^ flip]) for places in PLACES for p in range(64)]
    return lax.ppermute(block, CHIPS, pairs)


def spread(pieces):
    return lax.all_to_all(
        pieces, CHIPS, split_axis=0, concat_axis=0, tiled=True, axis_index_groups=PLACES
    )


def project(attn_out, w_proj, beside):
    rows, cols = attn_out.shape[0], w_proj.shape[1]
    core = lax.axis_index("core")
    me = (lax.axis_index(("yl", "xl")) ^ (core * 3)).reshape(1).astype(jnp.int32)
    sent, *blocks = prepare(me, attn_out, w_proj.T)
    tokens = spread(sent)
    for d in range(1, 4):
        blocks[d] = trade(blocks[d], d)
    lane = jnp.arange(4 * cols, dtype=jnp.int32)
    moves = jnp.broadcast_to((lane >= 2 * cols) & (core == 1), (rows, 4 * cols))
    tokens, beside, moves = lax.optimization_barrier((tokens, beside, moves))
    partial = partial_sums(me, tokens.reshape(64 * rows, -1), blocks)
    got = spread(partial.reshape(64, rows, -1))
    got = got.reshape(4, 2, 4, 2, rows, -1)[..., : 4 * cols].astype(F32)
    got = jnp.sum(got, axis=(1, 3)).astype(BF16)
    got = jnp.where(moves, jnp.roll(got, 1, axis=0), got)
    got = lax.all_to_all(got, "tensor", split_axis=0, concat_axis=0, tiled=True)
    total = jnp.sum(got.astype(F32), axis=0).astype(BF16)
    total = total.reshape(4, rows, 2, 2, cols).transpose(1, 2, 0, 3, 4).reshape(rows, 2, 8, cols)
    total = jnp.where(core == 1, jnp.roll(total[:, ::-1], 1, axis=2), total)
    return lax.optimization_barrier(total.reshape(rows, 16 * cols)), beside


def per_device(attn_out, w_proj, w_in, w_out, expert_ids, slots, gates):
    groups = lax.axis_size(EXPERT)
    width_block = w_in.shape[1]
    slice_units = w_in.shape[3]
    row = jnp.arange(groups * CAP, dtype=jnp.int32)
    matches = (expert_ids[:, :, None] == row // (HSPLIT * CAP)) & (slots[:, :, None] == row % CAP)
    dispatch_w = jnp.sum(matches.astype(F32), axis=1).astype(BF16)
    combine_w = jnp.sum(jnp.where(matches, gates[:, :, None], F32(0.0)), axis=1)
    beside = (w_in.reshape(width_block, 2 * slice_units), dispatch_w.T, combine_w)
    projected, (gate_up_w, dispatch_w, combine_w) = project(attn_out, w_proj, beside)
    outgoing = jnp.einsum(
        "gct,td->gcd",
        dispatch_w.reshape(groups, CAP, -1),
        projected,
        preferred_element_type=F32,
    ).astype(BF16)
    down_w = w_out.reshape(slice_units, width_block)
    projected, outgoing = lax.optimization_barrier((projected, outgoing))
    received = lax.all_to_all(outgoing, EXPERT, split_axis=0, concat_axis=0, tiled=True)
    flat_rows = received.reshape(groups * CAP, width_block)
    gate_up = gate_up_product(flat_rows, gate_up_w)
    quarter = groups * CAP // 4
    gate_up = lax.all_to_all(
        gate_up.reshape(4, quarter, 2 * slice_units), "tensor", split_axis=0, concat_axis=0, tiled=True
    )
    gate_up = jnp.sum(gate_up.astype(F32), axis=0)
    hidden = (jax.nn.silu(gate_up[:, :slice_units]) * gate_up[:, slice_units:]).astype(BF16)
    hidden = lax.all_to_all(
        jnp.broadcast_to(hidden[None], (4, quarter, slice_units)),
        "tensor",
        split_axis=0,
        concat_axis=0,
        tiled=True,
    ).reshape(groups * CAP, slice_units)
    result = jnp.dot(hidden, down_w, preferred_element_type=F32)
    returned = lax.all_to_all(
        result.reshape(groups, CAP, width_block).astype(BF16),
        EXPERT,
        split_axis=0,
        concat_axis=0,
        tiled=True,
    ).reshape(groups * CAP, width_block)
    moe_out = jnp.dot(
        combine_w, returned.astype(F32), precision=lax.Precision.HIGHEST, preferred_element_type=F32
    )
    return (projected, moe_out.astype(BF16))


def solution(mesh):
    split = Mesh(
        mesh.devices.reshape(2, 2, 4, 2, 4, 2, 4),
        ("plane", "core", "yh", "yl", "xh", "xl", "tensor"),
    )
    rows = ("plane", "core") + EXPERT
    placed = (
        P(rows, "tensor"),
        P("tensor", EXPERT),
        P(EXPERT, "tensor", None, None),
        P(EXPERT, None, "tensor"),
        P(rows, None),
        P(rows, None),
        P(rows, None),
    )
    return jax.shard_map(
        per_device,
        mesh=split,
        in_specs=placed,
        out_specs=(P(rows, "tensor"), P(rows, "tensor")),
        check_vma=False,
    )
```

```python
import jax
import jax.numpy as jnp
from jax import lax
from jax.experimental import pallas as pl
from jax.experimental.pallas import tpu as pltpu
from jax.sharding import Mesh, PartitionSpec as P

HSPLIT = 4
CAP = 2
EXPERT = ("yh", "yl", "xh", "xl")
BF16 = jnp.bfloat16
F32 = jnp.float32


VMEM = pl.BlockSpec(memory_space=pltpu.VMEM)
SMEM = pl.BlockSpec(memory_space=pltpu.SMEM)
ANY = pl.BlockSpec(memory_space=pl.ANY)


def address_kernel(attn_ref, sent_ref, staged, in_sems, out_sems):
    part = attn_ref.shape[1] // 4
    copies = []
    for m in range(4):
        for x in range(4):
            at = (m // 2) * 8 + x * 2 + m % 2
            copies.append(
                pltpu.make_async_copy(
                    attn_ref.at[:, pl.ds(m * part, part)], staged.at[at], in_sems.at[at]
                )
            )
    for copy in copies:
        copy.start()
    for copy in copies:
        copy.wait()
    copies = [
        pltpu.make_async_copy(staged, sent_ref.at[pl.ds(yh * 16, 16)], out_sems.at[yh])
        for yh in range(4)
    ]
    for copy in copies:
        copy.start()
    for copy in copies:
        copy.wait()


def address(attn_out):
    rows, part = attn_out.shape[0], attn_out.shape[1] // 4
    return pl.pallas_call(
        address_kernel,
        out_shape=jax.ShapeDtypeStruct((64, rows, part), BF16),
        in_specs=[ANY],
        out_specs=ANY,
        scratch_shapes=[
            pltpu.VMEM((16, rows, part), BF16),
            pltpu.SemaphoreType.DMA((16,)),
            pltpu.SemaphoreType.DMA((4,)),
        ],
        compiler_params=pltpu.CompilerParams(vmem_limit_bytes=58 << 20),
        name="address",
    )(attn_out)


PARTNERS = (0, 3, 1, 2)


def cut_kernel(me, w_ref, *pieces):
    part = pieces[0].shape[1]
    for i, d in enumerate(PARTNERS):
        start = pl.multiple_of((me[0] ^ d) * part, part)
        pieces[i][...] = w_ref[:, pl.ds(start, part)]


def cut(me, w_cols):
    cols, part = w_cols.shape[0], w_cols.shape[1] // 4
    return pl.pallas_call(
        cut_kernel,
        out_shape=[jax.ShapeDtypeStruct((cols, part), BF16)] * 4,
        in_specs=[SMEM, VMEM],
        out_specs=[VMEM] * 4,
        compiler_params=pltpu.CompilerParams(vmem_limit_bytes=8 << 20),
        name="cut",
    )(me, w_cols)


def partial_kernel(me, tokens, *refs):
    blocks, (out_ref, wide) = refs[:4], refs[4:]
    cols = blocks[0].shape[0]
    spare = wide.shape[0] - 4 * cols
    wide[pl.ds(4 * cols, spare), :] = jnp.zeros((spare, wide.shape[1]), BF16)
    for i, d in enumerate(PARTNERS):
        wide[pl.ds(pl.multiple_of((me[0] ^ d) * cols, 16), cols), :] = blocks[i][...]
    out_ref[...] = lax.dot_general(
        tokens[...], wide[...], (((1,), (1,)), ((), ())), preferred_element_type=F32
    ).astype(BF16)


def partial_sums(me, tokens, blocks):
    cols, part = blocks[0].shape
    padded = -(-4 * cols // 128) * 128
    return pl.pallas_call(
        partial_kernel,
        out_shape=jax.ShapeDtypeStruct((tokens.shape[0], padded), BF16),
        in_specs=[SMEM] + [VMEM] * 5,
        out_specs=VMEM,
        scratch_shapes=[pltpu.VMEM((padded, part), BF16)],
        compiler_params=pltpu.CompilerParams(vmem_limit_bytes=16 << 20),
        name="partial_sums",
    )(me, tokens, *blocks)


CHIPS = ("core",) + EXPERT
PLACES = [
    [64 * core + (y + core) % 8 * 8 + (x + core) % 8 for y in range(8) for x in range(8)]
    for core in range(2)
]


def trade(block, d):
    flip = (d // 2) * 8 + d % 2
    pairs = [(places[p], places[p ^ flip]) for places in PLACES for p in range(64)]
    return lax.ppermute(block, CHIPS, pairs)


def spread(pieces):
    return lax.all_to_all(
        pieces, CHIPS, split_axis=0, concat_axis=0, tiled=True, axis_index_groups=PLACES
    )


def project(attn_out, w_proj, beside):
    rows, cols = attn_out.shape[0], w_proj.shape[1]
    core = lax.axis_index("core")
    me = (lax.axis_index(("yl", "xl")) ^ (core * 3)).reshape(1).astype(jnp.int32)
    tokens = spread(address(attn_out))
    blocks = list(cut(me, w_proj.T))
    for i in range(1, 4):
        blocks[i] = trade(blocks[i], PARTNERS[i])
    lane = jnp.arange(4 * cols, dtype=jnp.int32)
    moves = jnp.broadcast_to((lane >= 2 * cols) & (core == 1), (rows, 4 * cols))
    tokens, beside, moves = lax.optimization_barrier((tokens, beside, moves))
    partial = partial_sums(me, tokens.reshape(64 * rows, -1), blocks)
    got = spread(partial.reshape(64, rows, -1))
    got = got.reshape(4, 2, 4, 2, rows, -1)[..., : 4 * cols].astype(F32)
    got = jnp.sum(got, axis=(1, 3)).astype(BF16)
    got = jnp.where(moves, jnp.roll(got, 1, axis=0), got)
    got = lax.all_to_all(got, "tensor", split_axis=0, concat_axis=0, tiled=True)
    total = jnp.sum(got.astype(F32), axis=0).astype(BF16)
    total = total.reshape(4, rows, 2, 2, cols).transpose(1, 2, 0, 3, 4).reshape(rows, 2, 8, cols)
    total = jnp.where(core == 1, jnp.roll(total[:, ::-1], 1, axis=2), total)
    return lax.optimization_barrier(total.reshape(rows, 16 * cols)), beside


def per_device(attn_out, w_proj, w_in, w_out, expert_ids, slots, gates):
    groups = lax.axis_size(EXPERT)
    width_block = w_in.shape[1]
    slice_units = w_in.shape[3]
    row = jnp.arange(groups * CAP, dtype=jnp.int32)
    matches = (expert_ids[:, :, None] == row // (HSPLIT * CAP)) & (slots[:, :, None] == row % CAP)
    dispatch_w = jnp.sum(matches.astype(F32), axis=1).astype(BF16)
    combine_w = jnp.sum(jnp.where(matches, gates[:, :, None], F32(0.0)), axis=1)
    beside = (w_in.reshape(width_block, 2 * slice_units), dispatch_w.T, combine_w)
    projected, (gate_up_w, dispatch_w, combine_w) = project(attn_out, w_proj, beside)
    outgoing = jnp.einsum(
        "gct,td->gcd",
        dispatch_w.reshape(groups, CAP, -1),
        projected,
        preferred_element_type=F32,
    ).astype(BF16)
    down_w = w_out.reshape(slice_units, width_block)
    projected, outgoing = lax.optimization_barrier((projected, outgoing))
    received = lax.all_to_all(outgoing, EXPERT, split_axis=0, concat_axis=0, tiled=True)
    flat_rows = received.reshape(groups * CAP, width_block)
    gate_up = jnp.dot(flat_rows, gate_up_w, preferred_element_type=F32).astype(BF16)
    quarter = groups * CAP // 4
    gate_up = lax.all_to_all(
        gate_up.reshape(4, quarter, 2 * slice_units), "tensor", split_axis=0, concat_axis=0, tiled=True
    )
    gate_up = jnp.sum(gate_up.astype(F32), axis=0)
    hidden = (jax.nn.silu(gate_up[:, :slice_units]) * gate_up[:, slice_units:]).astype(BF16)
    hidden = lax.all_to_all(
        jnp.broadcast_to(hidden[None], (4, quarter, slice_units)),
        "tensor",
        split_axis=0,
        concat_axis=0,
        tiled=True,
    ).reshape(groups * CAP, slice_units)
    result = jnp.dot(hidden, down_w, preferred_element_type=F32)
    returned = lax.all_to_all(
        result.reshape(groups, CAP, width_block).astype(BF16),
        EXPERT,
        split_axis=0,
        concat_axis=0,
        tiled=True,
    ).reshape(groups * CAP, width_block)
    moe_out = jnp.dot(
        combine_w, returned.astype(F32), precision=lax.Precision.HIGHEST, preferred_element_type=F32
    )
    return (projected, moe_out.astype(BF16))


def solution(mesh):
    split = Mesh(
        mesh.devices.reshape(2, 2, 4, 2, 4, 2, 4),
        ("plane", "core", "yh", "yl", "xh", "xl", "tensor"),
    )
    rows = ("plane", "core") + EXPERT
    placed = (
        P(rows, "tensor"),
        P("tensor", EXPERT),
        P(EXPERT, "tensor", None, None),
        P(EXPERT, None, "tensor"),
        P(rows, None),
        P(rows, None),
        P(rows, None),
    )
    return jax.shard_map(
        per_device,
        mesh=split,
        in_specs=placed,
        out_specs=(P(rows, "tensor"), P(rows, "tensor")),
        check_vma=False,
    )
```
